512 devices in a mesh: srv: 8 (over y_lo, core), trn: 64 (over x, z, y_hi).
Axes of the slice: x: 4, y: 8 (y_hi: 2, y_lo: 4; y = y_hi * 4 + y_lo), z: 8, core: 2. Of those that a mesh axis runs over, the one named last changes fastest.
Arguments:
- entities: float32 [400, 65536], P(None, ('trn', 'srv')), may hold values from -1.5 to 1.5
- entity_state: float32 [65536], P(('trn', 'srv')), may hold values from 0.05 to 0.5
- relations: float32 [2, 400, 400], replicated, may hold values from -0.3125 to 0.3125
- relation_state: float32 [2, 400], replicated, may hold values from 0.05 to 0.5
- heads: int32 [2, 131072], P(None, ('trn', 'srv')), may hold values from 0 to 1023
- tails: int32 [2, 131072], P(None, ('trn', 'srv')), may hold values from 0 to 1023
- rel_ids: int32 [2, 131072], P(None, ('trn', 'srv')), may hold values from 0 to 1
- negatives: int32 [2, 1024, 1024], P(None, ('trn', 'srv')), may hold values from 0 to 1023
Outputs:
- new_entities: float32 [400, 65536], P(None, ('trn', 'srv'))
- new_entity_state: float32 [65536], P(('trn', 'srv'))
- new_relations: float32 [2, 400, 400], replicated
- new_relation_state: float32 [2, 400], replicated
The draws below stay inside these ranges and needn't reach their ends.
Inputs may be any that keep to these rules, and one draw needn't show every extreme that they name: `heads`: indices within a partition of 1024 entities. `tails`: indices within a partition of 1024 entities. `negatives`: indices within the right partition of 1024 entities.
All inputs are finite; a program needn't handle non-finite values.
Results may differ from the reference program's by a relative error of at most 0.006.
Values may be sent and summed in bfloat16 or wider, within the bound.
No kernel may reach another device: no remote copies, remote signals or barrier semaphores. Data moves between devices by JAX's collectives and lax.ppermute only.
A program may use at most 64 MiB of HBM per device.

```python
import math
import jax
import jax.numpy as jnp
import numpy as np
from jax import lax

D = 400
RELS = 2
NEG = 1024
SPAN = 128
EDGE_DEV = 256
PART = 1024
ENTITIES = 65536
EDGES = 131072
SPANS = 1024
N_SRV = 8
N_TRN = 64


def place_ends(drawn, own_key, low, high):
    place = [jax.random.randint(jax.random.fold_in(own_key, axis), (), 0, length) for axis, length in enumerate(drawn.shape)]
    longest = drawn.shape.index(max(drawn.shape))
    next_to = place[:longest] + [(place[longest] + 1) % drawn.shape[longest]] + place[longest + 1:]
    return drawn.at[tuple(place)].set(low).at[tuple(next_to)].set(high)


def levels(stream_key, dims, split, least, top_value):
    level = 1.0
    for position, shards_of in split:
        heights = jax.random.uniform(jax.random.fold_in(jax.random.fold_in(stream_key, 6), position), (shards_of,), jnp.float32, least / len(split), top_value / len(split))
        level = level * jnp.repeat(jnp.exp(heights), dims[position] // shards_of).reshape((-1,) + (1,) * (len(dims) - 1 - position))
    return level


def cumulative_ranks(amount, slope):
    weights = [(1 << 20) // math.isqrt(standing ** slope) + 1 for standing in range(1, amount + 1)]
    width = 1 + sum(weights) // (1 << 30)
    return np.cumsum(np.array([max(1, weight // width) for weight in weights]))


def skewed_ids(own_key, extent, count, skew):
    listing = cumulative_ranks(count, skew)
    pick = jax.random.randint(jax.random.fold_in(own_key, 1), extent, 0, int(listing[count - 1]))
    grade = jnp.searchsorted(jnp.asarray(listing, jnp.int32), pick, side="right")
    return jax.random.permutation(jax.random.fold_in(own_key, 2), count)[grade].astype(jnp.int32)


def bell_draw(stream_key, extent, width, bound, pieces=(), kind=jnp.bfloat16):
    result = width * jax.random.normal(stream_key, extent, jnp.float32)
    if pieces:
        result = result * levels(stream_key, extent, pieces, -0.22, 0.18)
    return jnp.clip(result, -bound, bound).astype(kind)


def setup_inputs(seed: int = 0) -> dict:
    seeds = jax.random.split(jax.random.key(seed), 9)
    entities = bell_draw(seeds[0], (D, ENTITIES), 0.25, 1.5, ((1, 512),), jnp.float32)
    entity_state = jnp.clip(jnp.exp(math.log(0.5) - 2.3025851 * jax.random.uniform(seeds[1], (ENTITIES,), jnp.float32) ** levels(seeds[1], (ENTITIES,), ((0, 512),), -0.2, 0.2)), 0.05, 0.5)
    relations = bell_draw(seeds[2], (RELS, D, D), D ** -0.5, 0.3125, (), jnp.float32)
    relation_state = jnp.clip(jnp.exp(jax.random.uniform(seeds[3], (RELS, D), jnp.float32, math.log(0.05), math.log(0.5))), 0.05, 0.5)
    heads = place_ends(skewed_ids(seeds[4], (2, EDGES), PART, 2), jax.random.fold_in(seeds[4], 3), 0, PART - 1).astype(jnp.int32)
    tails = place_ends(jax.random.randint(seeds[5], (2, EDGES), 0, PART), jax.random.fold_in(seeds[5], 1), 0, PART - 1).astype(jnp.int32)
    rel_ids = place_ends(jax.random.randint(seeds[6], (2, EDGES), 0, RELS), jax.random.fold_in(seeds[6], 1), 0, RELS - 1).astype(jnp.int32)
    negatives = place_ends(jax.random.randint(seeds[7], (2, SPANS, NEG), 0, PART), jax.random.fold_in(seeds[7], 1), 0, PART - 1).astype(jnp.int32)
    return {"entities": entities, "entity_state": entity_state, "relations": relations, "relation_state": relation_state, "heads": heads, "tails": tails, "rel_ids": rel_ids, "negatives": negatives}


learn_rate = 0.1

def mult(form, left, right):
    return jnp.einsum(form, left.astype(jnp.float32), right.astype(jnp.float32), precision=lax.Precision.HIGHEST)

def bucket_grads(left, right, rel_b, head_idx, tail_idx, rel_idx, neg_idx):
    heads_cols = jnp.take(left, head_idx, axis=1)
    tails_cols = jnp.take(right, tail_idx, axis=1)
    masks = rel_idx[None, :] == jnp.arange(RELS, dtype=jnp.int32)[:, None]
    maskf = masks.astype(jnp.float32)
    query_all = mult('rdf,de->rfe', rel_b, heads_cols)
    query = lax.optimization_barrier(jnp.sum(query_all * maskf[:, None, :], axis=0)).astype(jnp.bfloat16)
    positive = lax.optimization_barrier(jnp.sum(query.astype(jnp.float32) * tails_cols.astype(jnp.float32), axis=0))
    grad_pos = -jax.nn.sigmoid(-positive)
    blocks = neg_idx.shape[0]
    query_blocks = query.reshape(D, blocks, SPAN).transpose(1, 0, 2)

    def one_block(carry, inputs):
        qblock, nidx = inputs
        negrows = jnp.take(right, nidx, axis=1)
        scores = mult('dk,dn->kn', qblock, negrows)
        weights = (jax.nn.sigmoid(scores) / NEG).astype(jnp.bfloat16)
        back = mult('dn,kn->dk', negrows, weights)
        rowgrad = mult('dk,kn->dn', qblock, weights)
        return (carry.at[:, nidx].add(rowgrad), back)
    grad_right, back_blocks = lax.scan(one_block, jnp.zeros((D, PART), jnp.float32), (query_blocks, neg_idx))
    back = back_blocks.transpose(1, 0, 2).reshape(D, blocks * SPAN)
    grad_query = grad_pos[None, :] * tails_cols.astype(jnp.float32) + back
    grad_right = grad_right.at[:, tail_idx].add(grad_pos[None, :] * query.astype(jnp.float32))
    gq_b = grad_query.astype(jnp.bfloat16)
    head_all = mult('rdf,fe->rde', rel_b, gq_b)
    grad_heads = lax.optimization_barrier(jnp.sum(head_all * maskf[:, None, :], axis=0))
    grad_left = jnp.zeros((D, PART), jnp.float32).at[:, head_idx].add(grad_heads)
    masked_heads = heads_cols[None, :, :] * masks[:, None, :].astype(jnp.bfloat16)
    grad_rel = mult('rde,fe->rdf', masked_heads, gq_b)
    return (grad_left, grad_right, grad_rel)

def reference(entities, entity_state, relations, relation_state, heads, tails, rel_ids, negatives):
    ent_b = entities.astype(jnp.bfloat16).reshape(D, N_TRN, PART).transpose(1, 0, 2)
    rel_b = relations.astype(jnp.bfloat16)
    per_bucket = N_SRV * EDGE_DEV
    heads_t = heads.reshape(2, N_TRN, per_bucket).transpose(1, 0, 2)
    tails_t = tails.reshape(2, N_TRN, per_bucket).transpose(1, 0, 2)
    rels_t = rel_ids.reshape(2, N_TRN, per_bucket).transpose(1, 0, 2)
    negs_t = negatives.reshape(2, N_TRN, per_bucket // SPAN, NEG).transpose(1, 0, 2, 3)
    prev_parts = jnp.roll(ent_b, 1, axis=0)

    def trainer(carry, inputs):
        own, prev, head_b, tail_b, rel_bk, neg_b = inputs
        left_one, right_one, rel_one = bucket_grads(own, own, rel_b, head_b[0], tail_b[0], rel_bk[0], neg_b[0])
        left_two, right_two, rel_two = bucket_grads(own, prev, rel_b, head_b[1], tail_b[1], rel_bk[1], neg_b[1])
        return (carry + rel_one + rel_two, (left_one + right_one + left_two, right_two))
    rel_grad, (grad_own, grad_prev) = lax.scan(trainer, jnp.zeros((RELS, D, D), jnp.float32), (ent_b, prev_parts, heads_t, tails_t, rels_t, negs_t))
    total = grad_own + jnp.roll(grad_prev, -1, axis=0)
    total = total.transpose(1, 0, 2).reshape(D, ENTITIES)
    new_state = entity_state + lax.optimization_barrier(jnp.mean(total * total, axis=0))
    new_entities = entities - learn_rate * total / jnp.sqrt(new_state)[None, :]
    new_rel_state = relation_state + lax.optimization_barrier(jnp.mean(rel_grad * rel_grad, axis=2))
    new_relations = relations - learn_rate * rel_grad / jnp.sqrt(new_rel_state)[:, :, None]
    return (new_entities, new_state, new_relations, new_rel_state)
```

```python
import functools

import jax
import jax.numpy as jnp
from jax import lax
from jax.experimental import pallas as pl
from jax.experimental.pallas import tpu as pltpu
from jax.sharding import Mesh, PartitionSpec as P

learn_rate = 0.1

D = 400
RELS = 2
NEG = 1024
SPAN = 128
EDGE = 256
PART = 1024
COLS = 128
SRV = ("yl", "core")
TRN = ("x", "z", "yh")
RING = ("x", "z")
COLUMN = ("yl", "yh")
STRIP = 56
REL_ROWS = 1280


def nn(a, b):
    return lax.dot_general(a, b, (((1,), (0,)), ((), ())), preferred_element_type=jnp.float32)


def nt(a, b):
    return lax.dot_general(a, b, (((1,), (1,)), ((), ())), preferred_element_type=jnp.float32)


def tn(a, b):
    return lax.dot_general(a, b, (((0,), (0,)), ((), ())), preferred_element_type=jnp.float32)


def one_hot(row, count):
    places = lax.broadcasted_iota(jnp.int32, (count, row.shape[1]), 0)
    return jnp.where(places == row, 1.0, 0.0).astype(jnp.bfloat16)


def neg_counts(row):
    high = one_hot(row // COLS, PART // COLS)
    low = one_hot(row % COLS, COLS)
    table = nt(high, low)
    return jnp.concatenate([table[i : i + 1, :] for i in range(PART // COLS)], axis=1)


def pack_relation(grad, out_ref, r):
    for group in range(3):
        out_ref[r, group * D : (group + 1) * D, :] = grad[:, group * COLS : (group + 1) * COLS]
    strip = grad[:, 3 * COLS :]
    packed = strip[:STRIP, :]
    for k in range(1, 8):
        piece = strip[k * STRIP : min((k + 1) * STRIP, D), :]
        if piece.shape[0] < STRIP:
            piece = jnp.concatenate([piece, jnp.zeros((STRIP - piece.shape[0], COLS), jnp.float32)], axis=0)
        packed = packed + pltpu.roll(piece, 16 * k, 1)
    out_ref[r, 3 * D : 3 * D + STRIP, :] = packed
    out_ref[r, 3 * D + STRIP :, :] = jnp.zeros((REL_ROWS - 3 * D - STRIP, COLS), jnp.float32)


def spread(grad, out_ref):
    for s in range(8):
        place = (s % 2) * 4 + s // 2
        out_ref[place * D : (place + 1) * D, :] = grad[:, s * COLS : (s + 1) * COLS].astype(jnp.bfloat16)


def buckets_kernel(parts_ref, rel_ref, heads_ref, tails_ref, rids_ref, negs_ref, own_ref, prev_ref, rel_out_ref):
    own = parts_ref[:D, :]
    rel = [rel_ref[r] for r in range(RELS)]
    heads, grads, masks, gleft, hots_h = [], [], [], [], []
    for b in range(2):
        right = own if b == 0 else parts_ref[D:, :]
        hot_h = one_hot(heads_ref[b : b + 1, :], PART)
        hot_t = one_hot(tails_ref[b : b + 1, :], PART)
        first = rids_ref[b : b + 1, :] == 0
        h = nn(own, hot_h).astype(jnp.bfloat16)
        t = nn(right, hot_t)
        q = jnp.where(first, tn(rel[0], h), tn(rel[1], h)).astype(jnp.bfloat16)
        qf = q.astype(jnp.float32)
        pos = jnp.sum(qf * t, axis=0, keepdims=True)
        gpos = -jax.nn.sigmoid(-pos)
        scores = tn(q, right)
        counts = [neg_counts(negs_ref[b, c : c + 1, :]) * (1.0 / NEG) for c in range(2)]
        weights = jnp.concatenate(
            [(jax.nn.sigmoid(scores[c * SPAN : (c + 1) * SPAN, :]) * counts[c]).astype(jnp.bfloat16) for c in range(2)],
            axis=0,
        )
        back = nt(right, weights)
        gq = (gpos * t + back).astype(jnp.bfloat16)
        gright = nn(q, weights) + nt((gpos * qf).astype(jnp.bfloat16), hot_t)
        gh = jnp.where(first, nn(rel[0], gq), nn(rel[1], gq)).astype(jnp.bfloat16)
        if b == 0:
            gown = gright
        else:
            spread(gright, prev_ref)
        heads.append(h)
        grads.append(gq)
        masks.append(first)
        gleft.append(gh)
        hots_h.append(hot_h)
    gown = gown + nt(jnp.concatenate(gleft, axis=1), jnp.concatenate(hots_h, axis=1))
    spread(gown, own_ref)
    h = jnp.concatenate(heads, axis=1)
    gq = jnp.concatenate([jnp.concatenate(grads, axis=1), jnp.zeros((512 - D, 2 * EDGE), jnp.bfloat16)], axis=0)
    first = jnp.concatenate(masks, axis=1)
    zero = jnp.zeros_like(h)
    pack_relation(nt(jnp.where(first, h, zero), gq), rel_out_ref, 0)
    pack_relation(nt(jnp.where(first, zero, h), gq), rel_out_ref, 1)


def relation_kernel(grad_ref, rel_ref, state_ref, rel_out_ref, state_out_ref):
    for r in range(RELS):
        base = r * REL_ROWS
        groups = [grad_ref[base + g * D : base + (g + 1) * D, :].astype(jnp.float32) for g in range(3)]
        packed = grad_ref[base + 3 * D : base + REL_ROWS, :].astype(jnp.float32)[:STRIP, :]
        pieces = []
        for k in range(8):
            piece = packed if k == 0 else pltpu.roll(packed, COLS - 16 * k, 1)
            pieces.append(piece if (k + 1) * STRIP <= D else piece[: D - k * STRIP, :])
        strip = jnp.concatenate(pieces, axis=0)[:, :16]
        squares = groups[0] * groups[0] + groups[1] * groups[1] + groups[2] * groups[2]
        mean = (jnp.sum(squares, axis=1, keepdims=True) + jnp.sum(strip * strip, axis=1, keepdims=True)) * (1.0 / D)
        across = jnp.transpose(jnp.broadcast_to(mean, (D, COLS)))[0:1, :]
        state = state_ref[r : r + 1, :] + across
        state_out_ref[r : r + 1, :] = state
        scale = jnp.transpose(jnp.broadcast_to(learn_rate * lax.rsqrt(state), (8, D)))[:, 0:1]
        for g in range(3):
            cols = slice(g * COLS, (g + 1) * COLS)
            rel_out_ref[r, :, cols] = rel_ref[r, :, cols] - groups[g] * scale
        rel_out_ref[r, :, 3 * COLS :] = rel_ref[r, :, 3 * COLS :] - strip * scale


def entity_kernel(own_ref, back_ref, ent_ref, state_ref, ent_out_ref, state_out_ref):
    total = back_ref[...].astype(jnp.float32)
    for k in range(4):
        total = total + own_ref[k * D : (k + 1) * D, :].astype(jnp.float32)
    state = state_ref[...] + jnp.sum(total * total, axis=0, keepdims=True) * (1.0 / D)
    state_out_ref[...] = state
    ent_out_ref[...] = ent_ref[...] - total * (learn_rate * lax.rsqrt(state))


def call(kernel, outs):
    return pl.pallas_call(
        kernel,
        out_shape=outs,
        compiler_params=pltpu.CompilerParams(vmem_limit_bytes=48 * 1024 * 1024),
    )


def shape(dims, dtype):
    return jax.ShapeDtypeStruct(dims, dtype)


def exchange(block, axis):
    return lax.all_to_all(block, axis, 0, 0, tiled=True)


def added(block, parts):
    return jnp.sum(block.astype(jnp.float32).reshape(parts, -1, COLS), axis=0)


def shards(entities, entity_state, relations, relation_state, heads, tails, rel_ids, negatives):
    bf = jnp.bfloat16
    own_b = entities.astype(bf)
    rel_b = relations.astype(bf)
    ahead = [(i, (i + 1) % 64) for i in range(64)]
    behind = [(i, (i - 1) % 64) for i in range(64)]
    prev_b = lax.ppermute(own_b, TRN, ahead)
    parts = lax.all_gather(jnp.concatenate([own_b, prev_b], axis=0), SRV, axis=1, tiled=True)
    gown, gprev, grel = call(
        buckets_kernel,
        (shape((8 * D, COLS), bf), shape((8 * D, COLS), bf), shape((RELS, REL_ROWS, COLS), jnp.float32)),
    )(parts, rel_b, heads, tails, rel_ids, negatives)

    rel = lax.psum_scatter(grel.reshape(RELS * REL_ROWS, COLS), "core", scatter_dimension=0, tiled=True)
    rel = added(exchange(rel.astype(bf), RING), 32).astype(bf)
    rel = added(exchange(jnp.tile(rel, (8, 1)), COLUMN), 8).astype(bf)
    rel = exchange(jnp.tile(rel, (32, 1)), RING)
    rel = lax.all_gather(rel, "core", axis=0, tiled=True)
    new_relations, new_rel_state = call(
        relation_kernel, (shape((RELS, D, D), jnp.float32), shape((RELS, D), jnp.float32))
    )(rel, relations, relation_state)

    gprev = lax.psum_scatter(gprev, "core", scatter_dimension=0, tiled=True)
    gprev = added(exchange(gprev, "yl"), 4).astype(bf)
    gprev = lax.ppermute(gprev, TRN, behind)
    gown = lax.psum_scatter(gown, "core", scatter_dimension=0, tiled=True)
    gown = exchange(gown, "yl")
    new_entities, new_state = call(
        entity_kernel, (shape((D, COLS), jnp.float32), shape((1, COLS), jnp.float32))
    )(gown, gprev, entities, entity_state.reshape(1, COLS))
    return (new_entities, new_state.reshape(COLS), new_relations, new_rel_state)


def solution(mesh):
    fine = Mesh(mesh.devices.reshape(4, 2, 4, 8, 2), ("yl", "core", "x", "z", "yh"))
    every = TRN + SRV
    in_specs = (P(None, every), P(every), P(), P(), P(None, every), P(None, every), P(None, every), P(None, every, None))
    out_specs = (P(None, every), P(every), P(), P())
    return jax.shard_map(shards, mesh=fine, in_specs=in_specs, out_specs=out_specs, check_vma=False)
```

```python
import jax
import jax.numpy as jnp
from jax import lax
from jax.experimental import pallas as pl
from jax.experimental.pallas import tpu as pltpu
from jax.sharding import Mesh, PartitionSpec as P

learn_rate = 0.1

D = 400
RELS = 2
NEG = 1024
SPAN = 128
EDGE = 256
PART = 1024
COLS = 128
SRV = ("yl", "core")
TRN = ("x", "z", "yh")
RING = ("x", "z")
COLUMN = ("yl", "yh")
STRIP = 56
REL_ROWS = 1280


def nn(a, b):
    return lax.dot_general(a, b, (((1,), (0,)), ((), ())), preferred_element_type=jnp.float32)


def nt(a, b):
    return lax.dot_general(a, b, (((1,), (1,)), ((), ())), preferred_element_type=jnp.float32)


def tn(a, b):
    return lax.dot_general(a, b, (((0,), (0,)), ((), ())), preferred_element_type=jnp.float32)


def one_hot(row, count):
    places = lax.broadcasted_iota(jnp.int32, (count, row.shape[1]), 0)
    return jnp.where(places == row, 1.0, 0.0).astype(jnp.bfloat16)


def neg_counts(row):
    high = one_hot(row // COLS, PART // COLS)
    low = one_hot(row % COLS, COLS)
    table = nt(high, low)
    return jnp.concatenate([table[i : i + 1, :] for i in range(PART // COLS)], axis=1)


def pack_relation(grad, out_ref):
    for group in range(3):
        out_ref[group * D : (group + 1) * D, :] = grad[:, group * COLS : (group + 1) * COLS]
    strip = grad[:, 3 * COLS :]
    packed = strip[:STRIP, :]
    for k in range(1, 8):
        piece = strip[k * STRIP : min((k + 1) * STRIP, D), :]
        if piece.shape[0] < STRIP:
            piece = jnp.concatenate([piece, jnp.zeros((STRIP - piece.shape[0], COLS), jnp.float32)], axis=0)
        packed = packed + pltpu.roll(piece, 16 * k, 1)
    out_ref[3 * D : 3 * D + STRIP, :] = packed
    out_ref[3 * D + STRIP :, :] = jnp.zeros((REL_ROWS - 3 * D - STRIP, COLS), jnp.float32)


def spread(grad, part, even, mine_ref, send_ref):
    for y in range(4):
        low = grad[:, 2 * y * COLS : (2 * y + 1) * COLS]
        high = grad[:, (2 * y + 1) * COLS : (2 * y + 2) * COLS]
        mine_ref[part, y] = jnp.where(even, low, high).astype(jnp.bfloat16)
        send_ref[part, y] = jnp.where(even, high, low).astype(jnp.bfloat16)


def buckets_kernel(
    core_ref, own_ref, prev_ref, rel_ref, heads_ref, tails_ref, rids_ref, negs_ref,
    rel_mine_ref, rel_send_ref, mine_ref, send_ref,
):
    core = core_ref[0]
    even = core == 0
    own = own_ref[...]
    rel = [rel_ref[r].astype(jnp.bfloat16) for r in range(RELS)]
    heads, grads, masks, gleft, hots_h = [], [], [], [], []
    for b in range(2):
        right = own if b == 0 else prev_ref[...]
        hot_h = one_hot(heads_ref[b : b + 1, :], PART)
        hot_t = one_hot(tails_ref[b : b + 1, :], PART)
        rids = rids_ref[b : b + 1, :]
        first = rids == 0
        h = nn(own, hot_h).astype(jnp.bfloat16)
        t = nn(right, hot_t)
        q = jnp.where(first, tn(rel[0], h), tn(rel[1], h)).astype(jnp.bfloat16)
        qf = q.astype(jnp.float32)
        pos = jnp.sum(qf * t, axis=0, keepdims=True)
        gpos = -jax.nn.sigmoid(-pos)
        scores = tn(q, right)
        counts = [neg_counts(negs_ref[b, c : c + 1, :]) * (1.0 / NEG) for c in range(2)]
        weights = jnp.concatenate(
            [(jax.nn.sigmoid(scores[c * SPAN : (c + 1) * SPAN, :]) * counts[c]).astype(jnp.bfloat16) for c in range(2)],
            axis=0,
        )
        back = nt(right, weights)
        gq = (gpos * t + back).astype(jnp.bfloat16)
        gright = nn(q, weights) + nt((gpos * qf).astype(jnp.bfloat16), hot_t)
        gh = jnp.where(first, nn(rel[0], gq), nn(rel[1], gq)).astype(jnp.bfloat16)
        if b == 0:
            gown = gright
        else:
            spread(gright, 1, even, mine_ref, send_ref)
        heads.append(h)
        grads.append(gq)
        masks.append(rids)
        gleft.append(gh)
        hots_h.append(hot_h)
    gown = gown + nt(jnp.concatenate(gleft, axis=1), jnp.concatenate(hots_h, axis=1))
    spread(gown, 0, even, mine_ref, send_ref)
    h = jnp.concatenate(heads, axis=1)
    gq = jnp.concatenate([jnp.concatenate(grads, axis=1), jnp.zeros((512 - D, 2 * EDGE), jnp.bfloat16)], axis=0)
    keep = jnp.concatenate(masks, axis=1) == core
    zero = jnp.zeros_like(h)
    pack_relation(nt(jnp.where(keep, h, zero), gq), rel_mine_ref)
    pack_relation(nt(jnp.where(keep, zero, h), gq), rel_send_ref)


def column_kernel(yl_ref, rel_mine_ref, rel_got_ref, mine_ref, got_ref, rel_ref, keep_ref, one_ref, two_ref, three_ref):
    rel_ref[...] = (rel_mine_ref[...] + rel_got_ref[...]).astype(jnp.bfloat16)
    for k, out_ref in enumerate((keep_ref, one_ref, two_ref, three_ref)):
        y = lax.rem(yl_ref[0] + k, 4)
        for part in range(2):
            total = mine_ref[part, y].astype(jnp.float32) + got_ref[part, y].astype(jnp.float32)
            out_ref[part] = total.astype(out_ref.dtype)


def ring_sum_kernel(got_ref, keep_ref, two_ref, out_ref, sum_ref):
    total = got_ref[0].astype(jnp.float32)
    for k in range(1, 32):
        total = total + got_ref[k].astype(jnp.float32)
    for k in range(8):
        out_ref[k] = total
    sum_ref[...] = keep_ref[...] + two_ref[...].astype(jnp.float32)


def column_sum_kernel(got_ref, sum_ref, one_ref, three_ref, rel_ref, own_ref, back_ref):
    total = got_ref[0]
    for k in range(1, 8):
        total = total + got_ref[k]
    total = total.astype(jnp.bfloat16)
    for k in range(32):
        rel_ref[k] = total
    own_ref[...] = sum_ref[0] + one_ref[0].astype(jnp.float32) + three_ref[0].astype(jnp.float32)
    back = sum_ref[1] + one_ref[1].astype(jnp.float32) + three_ref[1].astype(jnp.float32)
    back_ref[...] = back.astype(jnp.bfloat16)


def relation_kernel(grad_ref, rel_ref, state_ref, rel_out_ref, state_out_ref):
    for r in range(RELS):
        base = r * REL_ROWS
        groups = [grad_ref[base + g * D : base + (g + 1) * D, :].astype(jnp.float32) for g in range(3)]
        packed = grad_ref[base + 3 * D : base + REL_ROWS, :].astype(jnp.float32)[:STRIP, :]
        pieces = []
        for k in range(8):
            piece = packed if k == 0 else pltpu.roll(packed, COLS - 16 * k, 1)
            pieces.append(piece if (k + 1) * STRIP <= D else piece[: D - k * STRIP, :])
        strip = jnp.concatenate(pieces, axis=0)[:, :16]
        squares = groups[0] * groups[0] + groups[1] * groups[1] + groups[2] * groups[2]
        mean = (jnp.sum(squares, axis=1, keepdims=True) + jnp.sum(strip * strip, axis=1, keepdims=True)) * (1.0 / D)
        across = jnp.transpose(jnp.broadcast_to(mean, (D, COLS)))[0:1, :]
        state = state_ref[r : r + 1, :] + across
        state_out_ref[r : r + 1, :] = state
        scale = jnp.transpose(jnp.broadcast_to(learn_rate * lax.rsqrt(state), (8, D)))[:, 0:1]
        for g in range(3):
            cols = slice(g * COLS, (g + 1) * COLS)
            rel_out_ref[r, :, cols] = rel_ref[r, :, cols] - groups[g] * scale
        rel_out_ref[r, :, 3 * COLS :] = rel_ref[r, :, 3 * COLS :] - strip * scale


def entity_kernel(own_ref, back_ref, ent_ref, state_ref, ent_out_ref, state_out_ref):
    total = own_ref[...] + back_ref[...].astype(jnp.float32)
    state = state_ref[...] + jnp.sum(total * total, axis=0, keepdims=True) * (1.0 / D)
    state_out_ref[...] = state
    ent_out_ref[...] = ent_ref[...] - total * (learn_rate * lax.rsqrt(state))


VMEM = pl.BlockSpec(memory_space=pltpu.VMEM)
SMEM = pl.BlockSpec(memory_space=pltpu.SMEM)


def call(kernel, outs, scalars, arrays):
    return pl.pallas_call(
        kernel,
        out_shape=outs,
        in_specs=[SMEM] * scalars + [VMEM] * arrays,
        compiler_params=pltpu.CompilerParams(vmem_limit_bytes=48 * 1024 * 1024),
    )


def shape(dims, dtype):
    return jax.ShapeDtypeStruct(dims, dtype)


def exchange(block, axis):
    return lax.all_to_all(block, axis, 0, 0, tiled=True)


def shards(entities, entity_state, relations, relation_state, heads, tails, rel_ids, negatives):
    bf, f32 = jnp.bfloat16, jnp.float32
    core = lax.axis_index("core").astype(jnp.int32).reshape(1)
    yl = lax.axis_index("yl").astype(jnp.int32).reshape(1)
    own_b = entities.astype(bf)
    ahead = [(i, (i + 1) % 64) for i in range(64)]
    behind = [(i, (i - 1) % 64) for i in range(64)]
    swap = [(0, 1), (1, 0)]
    prev_b = lax.ppermute(own_b, TRN, ahead)
    own = lax.all_gather(own_b, SRV, axis=1, tiled=True)
    own, prev_b = lax.optimization_barrier((own, prev_b))
    prev = lax.all_gather(prev_b, SRV, axis=1, tiled=True)
    rel_shape, ent_shape = (REL_ROWS, COLS), (2, 4, D, COLS)
    rel_mine, rel_send, mine, send = call(
        buckets_kernel, (shape(rel_shape, f32), shape(rel_shape, f32), shape(ent_shape, bf), shape(ent_shape, bf)), 1, 7
    )(core, own, prev, relations, heads, tails, rel_ids, negatives)

    rel_got = lax.ppermute(rel_send, "core", swap)
    got = lax.ppermute(send, "core", swap)
    share = shape((2, D, COLS), bf)
    rel, keep, one, two, three = call(
        column_kernel, (shape(rel_shape, bf), shape((2, D, COLS), f32), share, share, share), 1, 4
    )(yl, rel_mine, rel_got, mine, got)

    piece = (REL_ROWS // 32, COLS)
    rel = exchange(rel.reshape(32, *piece), RING)
    one = lax.ppermute(one, "yl", [(i, (i + 1) % 4) for i in range(4)])
    two = lax.ppermute(two, "yl", [(i, (i + 2) % 4) for i in range(4)])
    three = lax.ppermute(three, "yl", [(i, (i + 3) % 4) for i in range(4)])
    ent = (2, D, COLS)
    rel, partial = call(ring_sum_kernel, (shape((8, *piece), f32), shape(ent, f32)), 0, 3)(rel, keep, two)
    rel = exchange(rel, COLUMN)
    rel, gown, back = call(
        column_sum_kernel, (shape((32, *piece), bf), shape((D, COLS), f32), shape((D, COLS), bf)), 0, 4
    )(rel, partial, one, three)

    rel = exchange(rel, RING)
    back = lax.ppermute(back, TRN, behind)
    rel = lax.all_gather(rel.reshape(rel_shape), "core", axis=0, tiled=True)
    new_relations, new_rel_state = call(relation_kernel, (shape((RELS, D, D), f32), shape((RELS, D), f32)), 0, 3)(
        rel, relations, relation_state
    )
    new_entities, new_state = call(entity_kernel, (shape((D, COLS), f32), shape((1, COLS), f32)), 0, 4)(
        gown, back, entities, entity_state.reshape(1, COLS)
    )
    return (new_entities, new_state.reshape(COLS), new_relations, new_rel_state)


def solution(mesh):
    fine = Mesh(mesh.devices.reshape(4, 2, 4, 8, 2), ("yl", "core", "x", "z", "yh"))
    every = TRN + SRV
    in_specs = (P(None, every), P(every), P(), P(), P(None, every), P(None, every), P(None, every), P(None, every, None))
    out_specs = (P(None, every), P(every), P(), P())
    return jax.shard_map(shards, mesh=fine, in_specs=in_specs, out_specs=out_specs, check_vma=False)
```

```python
import jax
import jax.numpy as jnp
from jax import lax
from jax.experimental import pallas as pl
from jax.experimental.pallas import tpu as pltpu
from jax.sharding import Mesh, PartitionSpec as P

learn_rate = 0.1

D = 400
RELS = 2
NEG = 1024
SPAN = 128
EDGE = 256
PART = 1024
COLS = 128
SRV = ("yl", "core")
TRN = ("x", "z", "yh")
STRIP = 56
REL_ROWS = 1280
PIECES = 64
PIECE = REL_ROWS // PIECES


def nn(a, b):
    return lax.dot_general(a, b, (((1,), (0,)), ((), ())), preferred_element_type=jnp.float32)


def nt(a, b):
    return lax.dot_general(a, b, (((1,), (1,)), ((), ())), preferred_element_type=jnp.float32)


def tn(a, b):
    return lax.dot_general(a, b, (((0,), (0,)), ((), ())), preferred_element_type=jnp.float32)


def one_hot(row, count):
    places = lax.broadcasted_iota(jnp.int32, (count, row.shape[1]), 0)
    return jnp.where(places == row, 1.0, 0.0).astype(jnp.bfloat16)


def neg_counts(row):
    high = one_hot(row // COLS, PART // COLS)
    low = one_hot(row % COLS, COLS)
    table = nt(high, low)
    return jnp.concatenate([table[i : i + 1, :] for i in range(PART // COLS)], axis=1)


def pack_relation(grad, out_ref):
    for group in range(3):
        out_ref[group * D : (group + 1) * D, :] = grad[:, group * COLS : (group + 1) * COLS].astype(out_ref.dtype)
    strip = grad[:, 3 * COLS :]
    packed = strip[:STRIP, :]
    for k in range(1, 8):
        piece = strip[k * STRIP : min((k + 1) * STRIP, D), :]
        if piece.shape[0] < STRIP:
            piece = jnp.concatenate([piece, jnp.zeros((STRIP - piece.shape[0], COLS), jnp.float32)], axis=0)
        packed = packed + pltpu.roll(piece, 16 * k, 1)
    packed = jnp.concatenate([packed, jnp.zeros((REL_ROWS - 3 * D - STRIP, COLS), jnp.float32)], axis=0)
    out_ref[3 * D : REL_ROWS, :] = packed.astype(out_ref.dtype)


def spread(grad, part, even, mine_ref, send_ref):
    for y in range(4):
        low = grad[:, 2 * y * COLS : (2 * y + 1) * COLS]
        high = grad[:, (2 * y + 1) * COLS : (2 * y + 2) * COLS]
        row = REL_ROWS + (part * 4 + y) * D
        mine_ref[part, y] = jnp.where(even, low, high).astype(jnp.bfloat16)
        send_ref[row : row + D, :] = jnp.where(even, high, low).astype(jnp.bfloat16)


def buckets_kernel(
    place_ref, own_ref, prev_ref, rel_ref, heads_ref, tails_ref, rids_ref, negs_ref, rel_mine_ref, mine_ref, send_ref
):
    yl, core = place_ref[0], place_ref[1]
    even = core == 0
    own = own_ref[...]
    rel = [rel_ref[r].astype(jnp.bfloat16) for r in range(RELS)]
    heads, grads, masks, gleft, hots_h = [], [], [], [], []
    for b in range(2):
        if b == 0:
            right = own
        else:
            blocks = []
            for i in range(4):
                m = lax.rem(yl + 4 - i, 4)
                at = lax.rem(m, 2) * 2 + m // 2
                blocks += [prev_ref[at, 0], prev_ref[at, 1]]
            right = jnp.concatenate(blocks, axis=1)
        hot_h = one_hot(heads_ref[b : b + 1, :], PART)
        hot_t = one_hot(tails_ref[b : b + 1, :], PART)
        rids = rids_ref[b : b + 1, :]
        first = rids == 0
        h = nn(own, hot_h).astype(jnp.bfloat16)
        t = nn(right, hot_t)
        q = jnp.where(first, tn(rel[0], h), tn(rel[1], h)).astype(jnp.bfloat16)
        qf = q.astype(jnp.float32)
        pos = jnp.sum(qf * t, axis=0, keepdims=True)
        gpos = -jax.nn.sigmoid(-pos)
        scores = tn(q, right)
        counts = [neg_counts(negs_ref[b, c : c + 1, :]) * (1.0 / NEG) for c in range(2)]
        weights = jnp.concatenate(
            [(jax.nn.sigmoid(scores[c * SPAN : (c + 1) * SPAN, :]) * counts[c]).astype(jnp.bfloat16) for c in range(2)],
            axis=0,
        )
        back = nt(right, weights)
        gq = (gpos * t + back).astype(jnp.bfloat16)
        gright = nn(q, weights) + nt((gpos * qf).astype(jnp.bfloat16), hot_t)
        gh = jnp.where(first, nn(rel[0], gq), nn(rel[1], gq)).astype(jnp.bfloat16)
        if b == 0:
            gown = gright
        else:
            spread(gright, 1, even, mine_ref, send_ref)
        heads.append(h)
        grads.append(gq)
        masks.append(rids)
        gleft.append(gh)
        hots_h.append(hot_h)
    gown = gown + nt(jnp.concatenate(gleft, axis=1), jnp.concatenate(hots_h, axis=1))
    spread(gown, 0, even, mine_ref, send_ref)
    h = jnp.concatenate(heads, axis=1)
    gq = jnp.concatenate([jnp.concatenate(grads, axis=1), jnp.zeros((512 - D, 2 * EDGE), jnp.bfloat16)], axis=0)
    keep = jnp.concatenate(masks, axis=1) == core
    zero = jnp.zeros_like(h)
    pack_relation(nt(jnp.where(keep, h, zero), gq), rel_mine_ref)
    pack_relation(nt(jnp.where(keep, zero, h), gq), send_ref)


def column_kernel(place_ref, rel_mine_ref, mine_ref, got_ref, rel_ref, keep_ref, one_ref, two_ref, three_ref, rows_ref):
    rows_ref[...] = rel_mine_ref[...] + got_ref[:REL_ROWS, :].astype(jnp.float32)
    for p in range(PIECES):
        rel_ref[p] = rows_ref[p * PIECE : (p + 1) * PIECE, :].astype(jnp.bfloat16)
    for k, out_ref in enumerate((keep_ref, one_ref, two_ref, three_ref)):
        y = lax.rem(place_ref[0] + k, 4)
        for part in range(2):
            row = pl.multiple_of(REL_ROWS + (part * 4 + y) * D, 16)
            total = mine_ref[part, y].astype(jnp.float32) + got_ref[pl.ds(row, D), :].astype(jnp.float32)
            out_ref[part] = total.astype(out_ref.dtype)


def trn_sum_kernel(got_ref, keep_ref, one_ref, two_ref, out_ref, sum_ref):
    total = got_ref[0].astype(jnp.float32)
    for k in range(1, PIECES):
        total = total + got_ref[k].astype(jnp.float32)
    for k in range(4):
        out_ref[k] = total
    sum_ref[...] = keep_ref[...] + one_ref[...].astype(jnp.float32) + two_ref[...].astype(jnp.float32)


def line_sum_kernel(got_ref, sum_ref, three_ref, rel_ref, own_ref, back_ref):
    total = got_ref[0]
    for k in range(1, 4):
        total = total + got_ref[k]
    total = total.astype(jnp.bfloat16)
    for k in range(PIECES):
        rel_ref[k] = total
    own_ref[...] = sum_ref[0] + three_ref[0].astype(jnp.float32)
    back_ref[...] = (sum_ref[1] + three_ref[1].astype(jnp.float32)).astype(jnp.bfloat16)


def relation_kernel(grad_ref, rel_ref, state_ref, rel_out_ref, state_out_ref, rows_ref):
    for r in range(RELS):
        rows_ref[...] = grad_ref[r].astype(jnp.float32)
        groups = [rows_ref[g * D : (g + 1) * D, :] for g in range(3)]
        packed = rows_ref[3 * D : 3 * D + STRIP, :]
        pieces = []
        for k in range(8):
            piece = packed if k == 0 else pltpu.roll(packed, COLS - 16 * k, 1)
            pieces.append(piece if (k + 1) * STRIP <= D else piece[: D - k * STRIP, :])
        strip = jnp.concatenate(pieces, axis=0)[:, :16]
        squares = groups[0] * groups[0] + groups[1] * groups[1] + groups[2] * groups[2]
        mean = (jnp.sum(squares, axis=1, keepdims=True) + jnp.sum(strip * strip, axis=1, keepdims=True)) * (1.0 / D)
        across = jnp.transpose(jnp.broadcast_to(mean, (D, COLS)))[0:1, :]
        state = state_ref[r : r + 1, :] + across
        state_out_ref[r : r + 1, :] = state
        scale = jnp.transpose(jnp.broadcast_to(learn_rate * lax.rsqrt(state), (8, D)))[:, 0:1]
        for g in range(3):
            cols = slice(g * COLS, (g + 1) * COLS)
            rel_out_ref[r, :, cols] = rel_ref[r, :, cols] - groups[g] * scale
        rel_out_ref[r, :, 3 * COLS :] = rel_ref[r, :, 3 * COLS :] - strip * scale


def entity_kernel(own_ref, back_ref, ent_ref, state_ref, ent_out_ref, state_out_ref):
    total = own_ref[...] + back_ref[...].astype(jnp.float32)
    state = state_ref[...] + jnp.sum(total * total, axis=0, keepdims=True) * (1.0 / D)
    state_out_ref[...] = state
    ent_out_ref[...] = ent_ref[...] - total * (learn_rate * lax.rsqrt(state))


VMEM = pl.BlockSpec(memory_space=pltpu.VMEM)
SMEM = pl.BlockSpec(memory_space=pltpu.SMEM)


def call(kernel, outs, scalars, arrays, scratch=()):
    return pl.pallas_call(
        kernel,
        out_shape=outs,
        in_specs=[SMEM] * scalars + [VMEM] * arrays,
        scratch_shapes=scratch,
        compiler_params=pltpu.CompilerParams(vmem_limit_bytes=48 * 1024 * 1024),
    )


def shape(dims, dtype):
    return jax.ShapeDtypeStruct(dims, dtype)


def exchange(block, axis):
    return lax.all_to_all(block, axis, 0, 0, tiled=True)


def onward(k):
    route = []
    for yl in range(4):
        for core in range(2):
            for t in range(64):
                to = (yl + 2 * k + core) % 4
                route.append(((yl * 2 + core) * 64 + t, (to * 2 + core) * 64 + (t + 1) % 64))
    return route


def shards(entities, entity_state, relations, relation_state, heads, tails, rel_ids, negatives):
    bf, f32 = jnp.bfloat16, jnp.float32
    place = jnp.stack([lax.axis_index("yl"), lax.axis_index("core")]).astype(jnp.int32)
    own_b = entities.astype(bf)
    chip_b = lax.all_gather(own_b, "core", axis=0, tiled=True)
    ahead = [lax.ppermute(chip_b, SRV + TRN, onward(k)) for k in range(2)]
    own = lax.all_gather(own_b, SRV, axis=1, tiled=True)
    own, *ahead = lax.optimization_barrier((own, *ahead))
    prev = lax.all_gather(jnp.concatenate(ahead, axis=0), "core", axis=0, tiled=True).reshape(4, 2, D, COLS)
    rel_mine, mine, send = call(
        buckets_kernel,
        (shape((REL_ROWS, COLS), f32), shape((2, 4, D, COLS), bf), shape((REL_ROWS + 8 * D, COLS), bf)),
        1,
        7,
    )(place, own, prev, relations, heads, tails, rel_ids, negatives)

    got = lax.ppermute(send, "core", [(0, 1), (1, 0)])
    share = shape((2, D, COLS), bf)
    total = shape((2, D, COLS), f32)
    pieces = shape((PIECES, PIECE, COLS), bf)
    rows = (pltpu.VMEM((REL_ROWS, COLS), f32),)
    rel, keep, one, two, three = call(column_kernel, (pieces, total, share, share, share), 1, 3, rows)(
        place, rel_mine, mine, got
    )

    rel = exchange(rel, TRN)
    one, two, three = [
        lax.ppermute(block, "yl", [(i, (i + k) % 4) for i in range(4)]) for k, block in ((1, one), (2, two), (3, three))
    ]
    rel, partial = call(trn_sum_kernel, (shape((4, PIECE, COLS), f32), total), 0, 4)(rel, keep, one, two)
    rel = exchange(rel, "yl")
    rel, gown, back = call(line_sum_kernel, (pieces, shape((D, COLS), f32), shape((D, COLS), bf)), 0, 3)(
        rel, partial, three
    )

    rel = exchange(rel, TRN)
    back = lax.ppermute(back, TRN, [(i, (i - 1) % 64) for i in range(64)])
    rel = lax.all_gather(rel.reshape(PIECES * PIECE, COLS), "core", axis=0, tiled=False)
    new_relations, new_rel_state = call(
        relation_kernel, (shape((RELS, D, D), f32), shape((RELS, D), f32)), 0, 3, rows
    )(rel, relations, relation_state)
    new_entities, new_state = call(entity_kernel, (shape((D, COLS), f32), shape((1, COLS), f32)), 0, 4)(
        gown, back, entities, entity_state.reshape(1, COLS)
    )
    return (new_entities, new_state.reshape(COLS), new_relations, new_rel_state)


def solution(mesh):
    fine = Mesh(mesh.devices.reshape(4, 2, 4, 8, 2), ("yl", "core", "x", "z", "yh"))
    every = TRN + SRV
    in_specs = (P(None, every), P(every), P(), P(), P(None, every), P(None, every), P(None, every), P(None, every, None))
    out_specs = (P(None, every), P(every), P(), P())
    return jax.shard_map(shards, mesh=fine, in_specs=in_specs, out_specs=out_specs, check_vma=False)
```

```python
import jax
import jax.numpy as jnp
from jax import lax
from jax.experimental import pallas as pl
from jax.experimental.pallas import tpu as pltpu
from jax.sharding import Mesh, PartitionSpec as P

learn_rate = 0.1

D = 400
RELS = 2
NEG = 1024
SPAN = 128
EDGE = 256
PART = 1024
COLS = 128
SRV = ("yl", "core")
TRN = ("x", "z", "yh")
STRIP = 56
REL_ROWS = 1280
PIECE = (REL_ROWS // 32, COLS)
RING = ("x", "z")
COLUMN = ("yl", "yh")


def nn(a, b):
    return lax.dot_general(a, b, (((1,), (0,)), ((), ())), preferred_element_type=jnp.float32)


def nt(a, b):
    return lax.dot_general(a, b, (((1,), (1,)), ((), ())), preferred_element_type=jnp.float32)


def tn(a, b):
    return lax.dot_general(a, b, (((0,), (0,)), ((), ())), preferred_element_type=jnp.float32)


def one_hot(row, count):
    places = lax.broadcasted_iota(jnp.int32, (count, row.shape[1]), 0)
    return jnp.where(places == row, 1.0, 0.0).astype(jnp.bfloat16)


def neg_counts(row):
    high = one_hot(row // COLS, PART // COLS)
    low = one_hot(row % COLS, COLS)
    table = nt(high, low)
    return jnp.concatenate([table[i : i + 1, :] for i in range(PART // COLS)], axis=1)


def pack_relation(grad, out_ref):
    for group in range(3):
        out_ref[group * D : (group + 1) * D, :] = grad[:, group * COLS : (group + 1) * COLS].astype(out_ref.dtype)
    strip = grad[:, 3 * COLS :]
    packed = strip[:STRIP, :]
    for k in range(1, 8):
        piece = strip[k * STRIP : min((k + 1) * STRIP, D), :]
        if piece.shape[0] < STRIP:
            piece = jnp.concatenate([piece, jnp.zeros((STRIP - piece.shape[0], COLS), jnp.float32)], axis=0)
        packed = packed + pltpu.roll(piece, 16 * k, 1)
    packed = jnp.concatenate([packed, jnp.zeros((REL_ROWS - 3 * D - STRIP, COLS), jnp.float32)], axis=0)
    out_ref[3 * D : REL_ROWS, :] = packed.astype(out_ref.dtype)


def spread(grad, part, even, mine_ref, send_ref):
    for y in range(4):
        low = grad[:, 2 * y * COLS : (2 * y + 1) * COLS]
        high = grad[:, (2 * y + 1) * COLS : (2 * y + 2) * COLS]
        mine_ref[part, y] = jnp.where(even, low, high).astype(jnp.bfloat16)
        send_ref[part, y] = jnp.where(even, high, low).astype(jnp.bfloat16)


def edge_grads(own, right, rel, b, heads_ref, tails_ref, rids_ref, negs_ref):
    first = rids_ref[b : b + 1, :] == 0
    h = nn(own, one_hot(heads_ref[b : b + 1, :], PART)).astype(jnp.bfloat16)
    t = nn(right, one_hot(tails_ref[b : b + 1, :], PART))
    q = jnp.where(first, tn(rel[0], h), tn(rel[1], h)).astype(jnp.bfloat16)
    qf = q.astype(jnp.float32)
    pos = jnp.sum(qf * t, axis=0, keepdims=True)
    gpos = -jax.nn.sigmoid(-pos)
    scores = tn(q, right)
    counts = [neg_counts(negs_ref[b, c : c + 1, :]) * (1.0 / NEG) for c in range(2)]
    weights = jnp.concatenate(
        [(jax.nn.sigmoid(scores[c * SPAN : (c + 1) * SPAN, :]) * counts[c]).astype(jnp.bfloat16) for c in range(2)],
        axis=0,
    )
    gq = (gpos * t + nt(right, weights)).astype(jnp.bfloat16)
    return h, q, (gpos * qf).astype(jnp.bfloat16), weights, gq


def right_grad(q, gpos_q, weights, tails):
    return nn(q, weights) + nt(gpos_q, one_hot(tails, PART))


def left_grad(gq, rel, rids, heads):
    gh = jnp.where(rids == 0, nn(rel[0], gq), nn(rel[1], gq)).astype(jnp.bfloat16)
    return nt(gh, one_hot(heads, PART))


def first_kernel(own_ref, rel_ref, heads_ref, tails_ref, rids_ref, negs_ref, rel_b_ref, h_ref, gq_ref, gown_ref):
    own = own_ref[...]
    rel = [rel_ref[r].astype(jnp.bfloat16) for r in range(RELS)]
    for r in range(RELS):
        rel_b_ref[r] = rel[r]
    h, q, gpos_q, weights, gq = edge_grads(own, own, rel, 0, heads_ref, tails_ref, rids_ref, negs_ref)
    h_ref[...] = h
    gq_ref[...] = gq
    gown_ref[...] = right_grad(q, gpos_q, weights, tails_ref[0:1, :]) + left_grad(
        gq, rel, rids_ref[0:1, :], heads_ref[0:1, :]
    )


def second_kernel(
    place_ref, own_ref, prev_ref, rel_ref, heads_ref, tails_ref, rids_ref, negs_ref, h_ref, gq_ref,
    rel_mine_ref, rel_send_ref, q_ref, gpos_q_ref, weights_ref, gq_two_ref,
):
    prev = jnp.concatenate([prev_ref[s % 2, s // 2] for s in range(8)], axis=1)
    h, q, gpos_q, weights, gq = edge_grads(own_ref[...], prev, rel_ref, 1, heads_ref, tails_ref, rids_ref, negs_ref)
    q_ref[...] = q
    gpos_q_ref[...] = gpos_q
    weights_ref[...] = weights
    gq_two_ref[...] = gq
    h = jnp.concatenate([h_ref[...], h], axis=1)
    gq = jnp.concatenate([gq_ref[...], gq], axis=1)
    gq = jnp.concatenate([gq, jnp.zeros((512 - D, 2 * EDGE), jnp.bfloat16)], axis=0)
    keep = jnp.concatenate([rids_ref[0:1, :], rids_ref[1:2, :]], axis=1) == place_ref[0]
    zero = jnp.zeros_like(h)
    pack_relation(nt(jnp.where(keep, h, zero), gq), rel_mine_ref)
    pack_relation(nt(jnp.where(keep, zero, h), gq), rel_send_ref)


def scatter_kernel(
    place_ref, rel_ref, heads_ref, tails_ref, rids_ref, q_ref, gpos_q_ref, weights_ref, gq_ref, gown_ref, mine_ref, send_ref
):
    even = place_ref[0] == 0
    gprev = right_grad(q_ref[...], gpos_q_ref[...], weights_ref[...], tails_ref[1:2, :])
    spread(gprev, 1, even, mine_ref, send_ref)
    gown = gown_ref[...] + left_grad(gq_ref[...], rel_ref, rids_ref[1:2, :], heads_ref[1:2, :])
    spread(gown, 0, even, mine_ref, send_ref)


def relation_add_kernel(mine_ref, got_ref, out_ref):
    out_ref[...] = (mine_ref[...] + got_ref[...].astype(jnp.float32)).astype(jnp.bfloat16)


def line_kernel(yl_ref, mine_ref, got_ref, keep_ref, one_ref, two_ref, three_ref):
    for k, out_ref in enumerate((keep_ref, one_ref, two_ref, three_ref)):
        y = lax.rem(yl_ref[0] + k, 4)
        for part in range(2):
            total = mine_ref[part, y].astype(jnp.float32) + got_ref[part, y].astype(jnp.float32)
            out_ref[part] = total.astype(out_ref.dtype)


def ring_sum_kernel(got_ref, keep_ref, one_ref, out_ref, sum_ref):
    total = got_ref[0].astype(jnp.float32)
    for k in range(1, 32):
        total = total + got_ref[k].astype(jnp.float32)
    for k in range(8):
        out_ref[k] = total
    sum_ref[...] = keep_ref[...] + one_ref[...].astype(jnp.float32)


def column_sum_kernel(got_ref, sum_ref, two_ref, three_ref, rel_ref, own_ref, back_ref):
    total = got_ref[0]
    for k in range(1, 8):
        total = total + got_ref[k]
    total = total.astype(jnp.bfloat16)
    for k in range(32):
        rel_ref[k] = total
    own_ref[...] = sum_ref[0] + two_ref[0].astype(jnp.float32) + three_ref[0].astype(jnp.float32)
    back = sum_ref[1] + two_ref[1].astype(jnp.float32) + three_ref[1].astype(jnp.float32)
    back_ref[...] = back.astype(jnp.bfloat16)


def relation_kernel(grad_ref, rel_ref, state_ref, rel_out_ref, state_out_ref):
    for r in range(RELS):
        base = r * REL_ROWS
        groups = [grad_ref[base + g * D : base + (g + 1) * D, :].astype(jnp.float32) for g in range(3)]
        packed = grad_ref[base + 3 * D : base + REL_ROWS, :].astype(jnp.float32)[:STRIP, :]
        pieces = []
        for k in range(8):
            piece = packed if k == 0 else pltpu.roll(packed, COLS - 16 * k, 1)
            pieces.append(piece if (k + 1) * STRIP <= D else piece[: D - k * STRIP, :])
        strip = jnp.concatenate(pieces, axis=0)[:, :16]
        squares = groups[0] * groups[0] + groups[1] * groups[1] + groups[2] * groups[2]
        mean = (jnp.sum(squares, axis=1, keepdims=True) + jnp.sum(strip * strip, axis=1, keepdims=True)) * (1.0 / D)
        across = jnp.transpose(jnp.broadcast_to(mean, (D, COLS)))[0:1, :]
        state = state_ref[r : r + 1, :] + across
        state_out_ref[r : r + 1, :] = state
        scale = jnp.transpose(jnp.broadcast_to(learn_rate * lax.rsqrt(state), (8, D)))[:, 0:1]
        for g in range(3):
            cols = slice(g * COLS, (g + 1) * COLS)
            rel_out_ref[r, :, cols] = rel_ref[r, :, cols] - groups[g] * scale
        rel_out_ref[r, :, 3 * COLS :] = rel_ref[r, :, 3 * COLS :] - strip * scale


def entity_kernel(own_ref, back_ref, ent_ref, state_ref, ent_out_ref, state_out_ref):
    total = own_ref[...] + back_ref[...].astype(jnp.float32)
    state = state_ref[...] + jnp.sum(total * total, axis=0, keepdims=True) * (1.0 / D)
    state_out_ref[...] = state
    ent_out_ref[...] = ent_ref[...] - total * (learn_rate * lax.rsqrt(state))


VMEM = pl.BlockSpec(memory_space=pltpu.VMEM)
SMEM = pl.BlockSpec(memory_space=pltpu.SMEM)


def call(kernel, outs, scalars, arrays, mib=8):
    return pl.pallas_call(
        kernel,
        out_shape=outs,
        in_specs=[SMEM] * scalars + [VMEM] * arrays,
        compiler_params=pltpu.CompilerParams(vmem_limit_bytes=mib * 1024 * 1024),
    )


def shape(dims, dtype):
    return jax.ShapeDtypeStruct(dims, dtype)


def exchange(block, axis):
    return lax.all_to_all(block, axis, 0, 0, tiled=True)


def shards(entities, entity_state, relations, relation_state, heads, tails, rel_ids, negatives):
    bf, f32 = jnp.bfloat16, jnp.float32
    core = lax.axis_index("core").astype(jnp.int32).reshape(1)
    yl = lax.axis_index("yl").astype(jnp.int32).reshape(1)
    swap = [(0, 1), (1, 0)]
    own_b = entities.astype(bf)
    prev_b = lax.ppermute(own_b, TRN, [(i, (i + 1) % 64) for i in range(64)])
    own = lax.all_gather(own_b, SRV, axis=1, tiled=True)
    own, prev_b = lax.optimization_barrier((own, prev_b))
    prev = exchange(jnp.tile(prev_b, (4, 1)), "yl")
    prev = lax.all_gather(prev, "core", axis=0, tiled=True).reshape(2, 4, D, COLS)

    edge = shape((D, EDGE), bf)
    rel_b, h, gq, gown = call(first_kernel, (shape((RELS, D, D), bf), edge, edge, shape((D, PART), f32)), 0, 6, 24)(
        own, relations, heads, tails, rel_ids, negatives
    )
    rel_shape, ent_shape = (REL_ROWS, COLS), shape((2, 4, D, COLS), bf)
    rel_mine, rel_send, q, gpos_q, weights, gq_two = call(
        second_kernel, (shape(rel_shape, f32), shape(rel_shape, bf), edge, edge, shape((EDGE, PART), bf), edge), 1, 9, 24
    )(core, own, prev, rel_b, heads, tails, rel_ids, negatives, h, gq)
    rel_got = lax.ppermute(rel_send, "core", swap)
    mine, send = call(scatter_kernel, (ent_shape, ent_shape), 1, 9, 24)(
        core, rel_b, heads, tails, rel_ids, q, gpos_q, weights, gq_two, gown
    )
    rel = call(relation_add_kernel, shape(rel_shape, bf), 0, 2)(rel_mine, rel_got)

    rel = exchange(rel.reshape(32, *PIECE), RING)
    got = lax.ppermute(send, "core", swap)
    share, total = shape((2, D, COLS), bf), shape((2, D, COLS), f32)
    keep, one, two, three = call(line_kernel, (total, share, share, share), 1, 2)(yl, mine, got)
    one, two, three = [
        lax.ppermute(block, "yl", [(i, (i + k) % 4) for i in range(4)]) for k, block in ((1, one), (2, two), (3, three))
    ]
    rel, partial = call(ring_sum_kernel, (shape((8, *PIECE), f32), total), 0, 3)(rel, keep, one)
    rel = exchange(rel, COLUMN)
    rel, gown, back = call(
        column_sum_kernel, (shape((32, *PIECE), bf), shape((D, COLS), f32), shape((D, COLS), bf)), 0, 4
    )(rel, partial, two, three)

    rel = exchange(rel, RING)
    back = lax.ppermute(back, TRN, [(i, (i - 1) % 64) for i in range(64)])
    rel = lax.all_gather(rel.reshape(rel_shape), "core", axis=0, tiled=True)
    new_relations, new_rel_state = call(relation_kernel, (shape((RELS, D, D), f32), shape((RELS, D), f32)), 0, 3)(
        rel, relations, relation_state
    )
    new_entities, new_state = call(entity_kernel, (shape((D, COLS), f32), shape((1, COLS), f32)), 0, 4)(
        gown, back, entities, entity_state.reshape(1, COLS)
    )
    return (new_entities, new_state.reshape(COLS), new_relations, new_rel_state)


def solution(mesh):
    fine = Mesh(mesh.devices.reshape(4, 2, 4, 8, 2), ("yl", "core", "x", "z", "yh"))
    every = TRN + SRV
    in_specs = (P(None, every), P(every), P(), P(), P(None, every), P(None, every), P(None, every), P(None, every, None))
    out_specs = (P(None, every), P(every), P(), P())
    return jax.shard_map(shards, mesh=fine, in_specs=in_specs, out_specs=out_specs, check_vma=False)
```

```python
import jax
import jax.numpy as jnp
from jax import lax
from jax.experimental import pallas as pl
from jax.experimental.pallas import tpu as pltpu
from jax.sharding import Mesh, PartitionSpec as P

learn_rate = 0.1

D = 400
RELS = 2
NEG = 1024
SPAN = 128
EDGE = 256
PART = 1024
COLS = 128
SRV = ("yl", "core")
TRN = ("x", "z", "yh")
STRIP = 56
REL_ROWS = 1280
PIECE = (REL_ROWS // 32, COLS)
RING = ("x", "z")
COLUMN = ("yl", "yh")


def nn(a, b):
    return lax.dot_general(a, b, (((1,), (0,)), ((), ())), preferred_element_type=jnp.float32)


def nt(a, b):
    return lax.dot_general(a, b, (((1,), (1,)), ((), ())), preferred_element_type=jnp.float32)


def tn(a, b):
    return lax.dot_general(a, b, (((0,), (0,)), ((), ())), preferred_element_type=jnp.float32)


def one_hot(row, count):
    places = lax.broadcasted_iota(jnp.int32, (count, row.shape[1]), 0)
    return jnp.where(places == row, 1.0, 0.0).astype(jnp.bfloat16)


def neg_counts(row):
    high = one_hot(row // COLS, PART // COLS)
    low = one_hot(row % COLS, COLS)
    table = nt(high, low)
    return jnp.concatenate([table[i : i + 1, :] for i in range(PART // COLS)], axis=1)


def pack_relation(grad, out_ref):
    for group in range(3):
        out_ref[group * D : (group + 1) * D, :] = grad[:, group * COLS : (group + 1) * COLS].astype(out_ref.dtype)
    strip = grad[:, 3 * COLS :]
    packed = strip[:STRIP, :]
    for k in range(1, 8):
        piece = strip[k * STRIP : min((k + 1) * STRIP, D), :]
        if piece.shape[0] < STRIP:
            piece = jnp.concatenate([piece, jnp.zeros((STRIP - piece.shape[0], COLS), jnp.float32)], axis=0)
        packed = packed + pltpu.roll(piece, 16 * k, 1)
    packed = jnp.concatenate([packed, jnp.zeros((REL_ROWS - 3 * D - STRIP, COLS), jnp.float32)], axis=0)
    out_ref[3 * D : REL_ROWS, :] = packed.astype(out_ref.dtype)


def edge_grads(h, right, rel, rids, tails, negs):
    first = rids == 0
    t = nn(right, one_hot(tails, PART))
    q = jnp.where(first, tn(rel[0], h), tn(rel[1], h)).astype(jnp.bfloat16)
    qf = q.astype(jnp.float32)
    pos = jnp.sum(qf * t, axis=0, keepdims=True)
    gpos = -jax.nn.sigmoid(-pos)
    scores = tn(q, right)
    weights = []
    for c, row in enumerate(negs):
        counts = neg_counts(row) * (1.0 / NEG)
        weights.append((jax.nn.sigmoid(scores[c * SPAN : (c + 1) * SPAN, :]) * counts).astype(jnp.bfloat16))
    weights = jnp.concatenate(weights, axis=0)
    gq = (gpos * t + nt(right, weights)).astype(jnp.bfloat16)
    return q, (gpos * qf).astype(jnp.bfloat16), weights, gq


def gather_heads(own, heads):
    return nn(own, one_hot(heads, PART)).astype(jnp.bfloat16)


def right_grad(q, gpos_q, weights, tails):
    return nn(q, weights) + nt(gpos_q, one_hot(tails, PART))


def left_grad(gq, rel, rids, heads):
    gh = jnp.where(rids == 0, nn(rel[0], gq), nn(rel[1], gq)).astype(jnp.bfloat16)
    return nt(gh, one_hot(heads, PART))


def heads_kernel(own_ref, heads_ref, h_ref):
    h_ref[...] = gather_heads(own_ref[...], heads_ref[1:2, :])


def index_kernel(tails_ref, rids_ref, negs_ref, index_ref):
    index_ref[0:1, :] = tails_ref[1:2, :]
    index_ref[1:2, :] = rids_ref[1:2, :]
    for c in range(2):
        for k in range(4):
            row = 2 + c * 4 + k
            index_ref[row : row + 1, :] = negs_ref[1, c : c + 1, k * EDGE : (k + 1) * EDGE]


def first_kernel(own_ref, rel_ref, heads_ref, tails_ref, rids_ref, negs_ref, rel_b_ref, h_ref, gq_ref, gown_ref):
    own = own_ref[...]
    rel = [rel_ref[r].astype(jnp.bfloat16) for r in range(RELS)]
    for r in range(RELS):
        rel_b_ref[r] = rel[r]
    heads, tails, rids = heads_ref[0:1, :], tails_ref[0:1, :], rids_ref[0:1, :]
    h = gather_heads(own, heads)
    q, gpos_q, weights, gq = edge_grads(h, own, rel, rids, tails, [negs_ref[0, c : c + 1, :] for c in range(2)])
    h_ref[...] = h
    gq_ref[...] = gq
    gown_ref[...] = right_grad(q, gpos_q, weights, tails) + left_grad(gq, rel, rids, heads)


def second_kernel(
    core_ref, own_ref, rel_ref, rids_ref, h_one_ref, gq_one_ref, h_two_ref, index_ref,
    rel_mine_ref, rel_send_ref, q_ref, gpos_q_ref, weights_ref, gq_ref,
):
    h = h_two_ref[...]
    tails, rids = index_ref[0:1, :], index_ref[1:2, :]
    negs = [jnp.concatenate([index_ref[2 + c * 4 + k : 3 + c * 4 + k, :] for k in range(4)], axis=1) for c in range(2)]
    q, gpos_q, weights, gq = edge_grads(h, own_ref[...], rel_ref, rids, tails, negs)
    q_ref[...] = q
    gpos_q_ref[...] = gpos_q
    weights_ref[...] = weights
    gq_ref[...] = gq
    h = jnp.concatenate([h_one_ref[...], h], axis=1)
    gq = jnp.concatenate([gq_one_ref[...], gq], axis=1)
    gq = jnp.concatenate([gq, jnp.zeros((512 - D, 2 * EDGE), jnp.bfloat16)], axis=0)
    keep = jnp.concatenate([rids_ref[0:1, :], rids], axis=1) == core_ref[0]
    zero = jnp.zeros_like(h)
    pack_relation(nt(jnp.where(keep, h, zero), gq), rel_mine_ref)
    pack_relation(nt(jnp.where(keep, zero, h), gq), rel_send_ref)


def relation_add_kernel(mine_ref, got_ref, out_ref):
    out_ref[...] = (mine_ref[...] + got_ref[...].astype(jnp.float32)).astype(jnp.bfloat16)


def ring_sum_kernel(got_ref, out_ref):
    total = got_ref[0].astype(jnp.float32)
    for k in range(1, 32):
        total = total + got_ref[k].astype(jnp.float32)
    for k in range(8):
        out_ref[k] = total


def scatter_kernel(
    core_ref, rel_ref, heads_ref, rids_ref, index_ref, gq_ref, q_hbm, gpos_q_hbm, weights_hbm, gown_hbm, _,
    mine_ref, send_ref, q_ref, gpos_q_ref, weights_ref, gown_ref, sems,
):
    even = core_ref[0] == 0
    held = ((q_hbm, q_ref), (gpos_q_hbm, gpos_q_ref), (weights_hbm, weights_ref), (gown_hbm, gown_ref))
    copies = [pltpu.make_async_copy(src, dst, sems.at[k]) for k, (src, dst) in enumerate(held)]
    for copy in copies:
        copy.start()
    grad = left_grad(gq_ref[...], rel_ref, rids_ref[1:2, :], heads_ref[1:2, :])
    for copy in copies:
        copy.wait()
    grad = grad + right_grad(q_ref[...], gpos_q_ref[...], weights_ref[...], index_ref[0:1, :]) + gown_ref[...]
    for y in range(4):
        low = grad[:, 2 * y * COLS : (2 * y + 1) * COLS]
        high = grad[:, (2 * y + 1) * COLS : (2 * y + 2) * COLS]
        mine_ref[y] = jnp.where(even, low, high).astype(jnp.bfloat16)
        send_ref[y] = jnp.where(even, high, low).astype(jnp.bfloat16)


def column_sum_kernel(yl_ref, rel_got_ref, mine_ref, got_ref, rel_ref, keep_ref, one_ref, two_ref, three_ref):
    total = rel_got_ref[0]
    for k in range(1, 8):
        total = total + rel_got_ref[k]
    total = total.astype(jnp.bfloat16)
    for k in range(32):
        rel_ref[k] = total
    for k, out_ref in enumerate((keep_ref, one_ref, two_ref, three_ref)):
        y = lax.rem(yl_ref[0] + k, 4)
        block = mine_ref[y].astype(jnp.float32) + got_ref[y].astype(jnp.float32)
        out_ref[...] = block.astype(out_ref.dtype)


def relation_kernel(grad_ref, rel_ref, state_ref, rel_out_ref, state_out_ref):
    for r in range(RELS):
        base = r * REL_ROWS
        groups = [grad_ref[base + g * D : base + (g + 1) * D, :].astype(jnp.float32) for g in range(3)]
        packed = grad_ref[base + 3 * D : base + REL_ROWS, :].astype(jnp.float32)[:STRIP, :]
        pieces = []
        for k in range(8):
            piece = packed if k == 0 else pltpu.roll(packed, COLS - 16 * k, 1)
            pieces.append(piece if (k + 1) * STRIP <= D else piece[: D - k * STRIP, :])
        strip = jnp.concatenate(pieces, axis=0)[:, :16]
        squares = groups[0] * groups[0] + groups[1] * groups[1] + groups[2] * groups[2]
        mean = (jnp.sum(squares, axis=1, keepdims=True) + jnp.sum(strip * strip, axis=1, keepdims=True)) * (1.0 / D)
        across = jnp.transpose(jnp.broadcast_to(mean, (D, COLS)))[0:1, :]
        state = state_ref[r : r + 1, :] + across
        state_out_ref[r : r + 1, :] = state
        scale = jnp.transpose(jnp.broadcast_to(learn_rate * lax.rsqrt(state), (8, D)))[:, 0:1]
        for g in range(3):
            cols = slice(g * COLS, (g + 1) * COLS)
            rel_out_ref[r, :, cols] = rel_ref[r, :, cols] - groups[g] * scale
        rel_out_ref[r, :, 3 * COLS :] = rel_ref[r, :, 3 * COLS :] - strip * scale


def entity_kernel(keep_ref, one_ref, two_ref, three_ref, ent_ref, state_ref, ent_out_ref, state_out_ref):
    total = keep_ref[...]
    for ref in (one_ref, two_ref, three_ref):
        total = total + ref[...].astype(jnp.float32)
    state = state_ref[...] + jnp.sum(total * total, axis=0, keepdims=True) * (1.0 / D)
    state_out_ref[...] = state
    ent_out_ref[...] = ent_ref[...] - total * (learn_rate * lax.rsqrt(state))


VMEM = pl.BlockSpec(memory_space=pltpu.VMEM)
SMEM = pl.BlockSpec(memory_space=pltpu.SMEM)


def call(kernel, outs, scalars, arrays, mib=8, hbm=0, scratch=()):
    return pl.pallas_call(
        kernel,
        out_shape=outs,
        in_specs=[SMEM] * scalars + [VMEM] * arrays + [pl.BlockSpec(memory_space=pltpu.HBM)] * hbm,
        scratch_shapes=scratch,
        compiler_params=pltpu.CompilerParams(vmem_limit_bytes=mib * 1024 * 1024),
    )


def shape(dims, dtype):
    return jax.ShapeDtypeStruct(dims, dtype)


def exchange(block, axis):
    return lax.all_to_all(block, axis, 0, 0, tiled=True)


def shards(entities, entity_state, relations, relation_state, heads, tails, rel_ids, negatives):
    bf, f32 = jnp.bfloat16, jnp.float32
    core = lax.axis_index("core").astype(jnp.int32).reshape(1)
    yl = lax.axis_index("yl").astype(jnp.int32).reshape(1)
    swap = [(0, 1), (1, 0)]
    before = [(i, (i - 1) % 64) for i in range(64)]
    after = [(i, (i + 1) % 64) for i in range(64)]
    edge = shape((D, EDGE), bf)

    own = lax.all_gather(entities.astype(bf), SRV, axis=1, tiled=True)
    h_two = lax.ppermute(call(heads_kernel, edge, 0, 2)(own, heads), TRN, before)
    index = call(index_kernel, shape((10, EDGE), jnp.int32), 0, 3)(tails, rel_ids, negatives)
    index = lax.ppermute(index, TRN, before)
    rel_b, h_one, gq_one, gown = call(first_kernel, (shape((RELS, D, D), bf), edge, edge, shape((D, PART), f32)), 0, 6, 24)(
        own, relations, heads, tails, rel_ids, negatives
    )
    rel_shape = (REL_ROWS, COLS)
    rel_mine, rel_send, q, gpos_q, weights, gq_two = call(
        second_kernel, (shape(rel_shape, f32), shape(rel_shape, bf), edge, edge, shape((EDGE, PART), bf), edge), 1, 7, 24
    )(core, own, rel_b, rel_ids, h_one, gq_one, h_two, index)
    rel_got = lax.ppermute(rel_send, "core", swap)
    gq_two = lax.ppermute(gq_two, TRN, after)
    rel = call(relation_add_kernel, shape(rel_shape, bf), 0, 2)(rel_mine, rel_got)

    rel = exchange(rel.reshape(32, *PIECE), RING)
    ring_sum = call(ring_sum_kernel, shape((8, *PIECE), f32), 0, 1)(rel)

    rel = exchange(ring_sum, COLUMN)
    half = shape((4, D, COLS), bf)
    held = [pltpu.VMEM((D, EDGE), bf)] * 2 + [pltpu.VMEM((EDGE, PART), bf), pltpu.VMEM((D, PART), f32)]
    held = (*held, pltpu.SemaphoreType.DMA((4,)))
    mine, send = call(scatter_kernel, (half, half), 1, 5, 58, 5, held)(
        core, rel_b, heads, rel_ids, index, gq_two, q, gpos_q, weights, gown, ring_sum
    )
    got = lax.ppermute(send, "core", swap)
    block, share = shape((D, COLS), f32), shape((D, COLS), bf)
    rel, keep, one, two, three = call(
        column_sum_kernel, (shape((32, *PIECE), bf), block, share, share, share), 1, 3
    )(yl, rel, mine, got)

    rel = exchange(rel, RING)
    one, two, three = [
        lax.ppermute(part, "yl", [(i, (i + k) % 4) for i in range(4)]) for k, part in ((1, one), (2, two), (3, three))
    ]
    new_entities, new_state = call(entity_kernel, (block, shape((1, COLS), f32)), 0, 6)(
        keep, one, two, three, entities, entity_state.reshape(1, COLS)
    )
    rel = lax.all_gather(rel.reshape(rel_shape), "core", axis=0, tiled=True)
    new_relations, new_rel_state = call(relation_kernel, (shape((RELS, D, D), f32), shape((RELS, D), f32)), 0, 3)(
        rel, relations, relation_state
    )
    return (new_entities, new_state.reshape(COLS), new_relations, new_rel_state)


def solution(mesh):
    fine = Mesh(mesh.devices.reshape(4, 2, 4, 8, 2), ("yl", "core", "x", "z", "yh"))
    every = TRN + SRV
    in_specs = (P(None, every), P(every), P(), P(), P(None, every), P(None, every), P(None, every), P(None, every, None))
    out_specs = (P(None, every), P(every), P(), P())
    return jax.shard_map(shards, mesh=fine, in_specs=in_specs, out_specs=out_specs, check_vma=False)
```

```python
import jax
import jax.numpy as jnp
from jax import lax
from jax.experimental import pallas as pl
from jax.experimental.pallas import tpu as pltpu
from jax.sharding import Mesh, PartitionSpec as P

learn_rate = 0.1

D = 400
RELS = 2
NEG = 1024
SPAN = 128
EDGE = 256
PART = 1024
COLS = 128
SRV = ("yl", "core")
TRN = ("x", "z", "yh")
STRIP = 56
CODES = 32
REL_ROWS = 1280
PIECE = (REL_ROWS // 32, COLS)
RING = ("x", "z")
COLUMN = ("yl", "yh")


def nn(a, b):
    return lax.dot_general(a, b, (((1,), (0,)), ((), ())), preferred_element_type=jnp.float32)


def nt(a, b):
    return lax.dot_general(a, b, (((1,), (1,)), ((), ())), preferred_element_type=jnp.float32)


def tn(a, b):
    return lax.dot_general(a, b, (((0,), (0,)), ((), ())), preferred_element_type=jnp.float32)


def one_hot(row, count):
    places = lax.broadcasted_iota(jnp.int32, (count, row.shape[1]), 0)
    return jnp.where(places == row, 1.0, 0.0).astype(jnp.bfloat16)


def neg_counts(row):
    high = one_hot(row // COLS, PART // COLS)
    low = one_hot(row % COLS, COLS)
    table = nt(high, low)
    return jnp.concatenate([table[i : i + 1, :] for i in range(PART // COLS)], axis=1)


def pack_relation(grad, out_ref):
    for group in range(3):
        out_ref[group * D : (group + 1) * D, :] = grad[:, group * COLS : (group + 1) * COLS].astype(out_ref.dtype)
    strip = grad[:, 3 * COLS :]
    packed = strip[:STRIP, :]
    for k in range(1, 8):
        piece = strip[k * STRIP : min((k + 1) * STRIP, D), :]
        if piece.shape[0] < STRIP:
            piece = jnp.concatenate([piece, jnp.zeros((STRIP - piece.shape[0], COLS), jnp.float32)], axis=0)
        packed = packed + pltpu.roll(piece, 16 * k, 1)
    packed = jnp.concatenate([packed, jnp.zeros((REL_ROWS - 3 * D - STRIP, COLS), jnp.float32)], axis=0)
    out_ref[3 * D : REL_ROWS, :] = packed.astype(out_ref.dtype)


def edge_grads(h, right, rel, rids, tails, negs):
    first = rids == 0
    t = nn(right, one_hot(tails, PART))
    q = jnp.where(first, tn(rel[0], h), tn(rel[1], h)).astype(jnp.bfloat16)
    qf = q.astype(jnp.float32)
    pos = jnp.sum(qf * t, axis=0, keepdims=True)
    gpos = -jax.nn.sigmoid(-pos)
    scores = tn(q, right)
    weights = []
    for c, row in enumerate(negs):
        counts = neg_counts(row) * (1.0 / NEG)
        weights.append((jax.nn.sigmoid(scores[c * SPAN : (c + 1) * SPAN, :]) * counts).astype(jnp.bfloat16))
    weights = jnp.concatenate(weights, axis=0)
    gq = (gpos * t + nt(right, weights)).astype(jnp.bfloat16)
    return q, (gpos * qf).astype(jnp.bfloat16), weights, gq


def gather_heads(own, heads):
    return nn(own, one_hot(heads, PART)).astype(jnp.bfloat16)


def right_grad(q, gpos_q, weights, tails):
    return nn(q, weights) + nt(gpos_q, one_hot(tails, PART))


def left_grad(gq, rel, rids, heads):
    gh = jnp.where(rids == 0, nn(rel[0], gq), nn(rel[1], gq)).astype(jnp.bfloat16)
    return nt(gh, one_hot(heads, PART))


def start_kernel(ent_ref, tails_ref, rids_ref, negs_ref, own_ref, code_ref):
    own_ref[...] = ent_ref[...].astype(jnp.bfloat16)
    rows = [tails_ref[1:2, :]]
    rows += [negs_ref[1, c : c + 1, k * EDGE : (k + 1) * EDGE] for c in range(2) for k in range(4)]
    rows = [part for row in rows for part in (row // 32, row % 32)] + [rids_ref[1:2, :]]
    rows.append(jnp.zeros((CODES - len(rows), EDGE), jnp.int32))
    code_ref[...] = jnp.concatenate([row.astype(jnp.float32) for row in rows], axis=0).astype(jnp.bfloat16)


def heads_kernel(own_ref, heads_ref, code_ref, out_ref):
    out_ref[:D, :] = gather_heads(own_ref[...], heads_ref[1:2, :])
    out_ref[D:, :] = code_ref[...]


def first_kernel(own_ref, rel_ref, heads_ref, tails_ref, rids_ref, negs_ref, rel_b_ref, h_ref, gq_ref, gown_ref):
    own = own_ref[...]
    rel = [rel_ref[r].astype(jnp.bfloat16) for r in range(RELS)]
    for r in range(RELS):
        rel_b_ref[r] = rel[r]
    heads, tails, rids = heads_ref[0:1, :], tails_ref[0:1, :], rids_ref[0:1, :]
    h = gather_heads(own, heads)
    q, gpos_q, weights, gq = edge_grads(h, own, rel, rids, tails, [negs_ref[0, c : c + 1, :] for c in range(2)])
    h_ref[...] = h
    gq_ref[...] = gq
    gown_ref[...] = right_grad(q, gpos_q, weights, tails) + left_grad(gq, rel, rids, heads)


def second_kernel(
    core_ref, own_ref, rel_ref, rids_ref, h_one_ref, gq_one_ref, two_ref,
    rel_mine_ref, rel_send_ref, q_ref, gpos_q_ref, weights_ref, gq_ref, tails_ref,
):
    h = two_ref[:D, :]
    code = two_ref[D:, :].astype(jnp.float32).astype(jnp.int32)
    rows = [code[2 * k : 2 * k + 1, :] * 32 + code[2 * k + 1 : 2 * k + 2, :] for k in range(9)]
    tails, rids = rows[0], code[18:19, :]
    negs = [jnp.concatenate(rows[1 + 4 * c : 5 + 4 * c], axis=1) for c in range(2)]
    tails_ref[...] = tails
    q, gpos_q, weights, gq = edge_grads(h, own_ref[...], rel_ref, rids, tails, negs)
    q_ref[...] = q
    gpos_q_ref[...] = gpos_q
    weights_ref[...] = weights
    gq_ref[...] = gq
    h = jnp.concatenate([h_one_ref[...], h], axis=1)
    gq = jnp.concatenate([gq_one_ref[...], gq], axis=1)
    gq = jnp.concatenate([gq, jnp.zeros((512 - D, 2 * EDGE), jnp.bfloat16)], axis=0)
    keep = jnp.concatenate([rids_ref[0:1, :], rids], axis=1) == core_ref[0]
    zero = jnp.zeros_like(h)
    pack_relation(nt(jnp.where(keep, h, zero), gq), rel_mine_ref)
    pack_relation(nt(jnp.where(keep, zero, h), gq), rel_send_ref)


def relation_add_kernel(mine_ref, got_ref, out_ref):
    out_ref[...] = (mine_ref[...] + got_ref[...].astype(jnp.float32)).astype(jnp.bfloat16)


def ring_sum_kernel(got_ref, out_ref):
    total = got_ref[0].astype(jnp.float32)
    for k in range(1, 32):
        total = total + got_ref[k].astype(jnp.float32)
    for k in range(8):
        out_ref[k] = total


def scatter_kernel(
    core_ref, rel_ref, heads_ref, rids_ref, tails_ref, gq_ref, q_hbm, gpos_q_hbm, weights_hbm, gown_hbm, _,
    mine_ref, send_ref, q_ref, gpos_q_ref, weights_ref, gown_ref, sems,
):
    even = core_ref[0] == 0
    held = ((q_hbm, q_ref), (gpos_q_hbm, gpos_q_ref), (weights_hbm, weights_ref), (gown_hbm, gown_ref))
    copies = [pltpu.make_async_copy(src, dst, sems.at[k]) for k, (src, dst) in enumerate(held)]
    for copy in copies:
        copy.start()
    grad = left_grad(gq_ref[...], rel_ref, rids_ref[1:2, :], heads_ref[1:2, :])
    for copy in copies:
        copy.wait()
    grad = grad + right_grad(q_ref[...], gpos_q_ref[...], weights_ref[...], tails_ref[...]) + gown_ref[...]
    for y in range(4):
        low = grad[:, 2 * y * COLS : (2 * y + 1) * COLS]
        high = grad[:, (2 * y + 1) * COLS : (2 * y + 2) * COLS]
        mine_ref[y] = jnp.where(even, low, high).astype(jnp.bfloat16)
        send_ref[y] = jnp.where(even, high, low).astype(jnp.bfloat16)


def column_sum_kernel(yl_ref, core_ref, rel_got_ref, mine_ref, got_ref, rel_ref, keep_ref, one_ref, two_ref, three_ref):
    total = rel_got_ref[0]
    for k in range(1, 8):
        total = total + rel_got_ref[k]
    total = total.astype(jnp.bfloat16)
    for k in range(32):
        rel_ref[k] = total
    for k, out_ref in enumerate((keep_ref, one_ref, two_ref, three_ref)):
        y = lax.rem(yl_ref[0] + k, 4)
        block = mine_ref[y].astype(jnp.float32) + got_ref[1 - core_ref[0], y].astype(jnp.float32)
        out_ref[...] = block.astype(out_ref.dtype)


def relation_kernel(grad_ref, rel_ref, state_ref, rel_out_ref, state_out_ref):
    for r in range(RELS):
        base = r * REL_ROWS
        groups = [grad_ref[base + g * D : base + (g + 1) * D, :].astype(jnp.float32) for g in range(3)]
        packed = grad_ref[base + 3 * D : base + REL_ROWS, :].astype(jnp.float32)[:STRIP, :]
        pieces = []
        for k in range(8):
            piece = packed if k == 0 else pltpu.roll(packed, COLS - 16 * k, 1)
            pieces.append(piece if (k + 1) * STRIP <= D else piece[: D - k * STRIP, :])
        strip = jnp.concatenate(pieces, axis=0)[:, :16]
        squares = groups[0] * groups[0] + groups[1] * groups[1] + groups[2] * groups[2]
        mean = (jnp.sum(squares, axis=1, keepdims=True) + jnp.sum(strip * strip, axis=1, keepdims=True)) * (1.0 / D)
        across = jnp.transpose(jnp.broadcast_to(mean, (D, COLS)))[0:1, :]
        state = state_ref[r : r + 1, :] + across
        state_out_ref[r : r + 1, :] = state
        scale = jnp.transpose(jnp.broadcast_to(learn_rate * lax.rsqrt(state), (8, D)))[:, 0:1]
        for g in range(3):
            cols = slice(g * COLS, (g + 1) * COLS)
            rel_out_ref[r, :, cols] = rel_ref[r, :, cols] - groups[g] * scale
        rel_out_ref[r, :, 3 * COLS :] = rel_ref[r, :, 3 * COLS :] - strip * scale


def entity_kernel(keep_ref, one_ref, two_ref, three_ref, ent_ref, state_ref, ent_out_ref, state_out_ref):
    total = keep_ref[...]
    for ref in (one_ref, two_ref, three_ref):
        total = total + ref[...].astype(jnp.float32)
    state = state_ref[...] + jnp.sum(total * total, axis=0, keepdims=True) * (1.0 / D)
    state_out_ref[...] = state
    ent_out_ref[...] = ent_ref[...] - total * (learn_rate * lax.rsqrt(state))


VMEM = pl.BlockSpec(memory_space=pltpu.VMEM)
SMEM = pl.BlockSpec(memory_space=pltpu.SMEM)


def call(kernel, outs, scalars, arrays, mib=8, hbm=0, scratch=()):
    return pl.pallas_call(
        kernel,
        out_shape=outs,
        in_specs=[SMEM] * scalars + [VMEM] * arrays + [pl.BlockSpec(memory_space=pltpu.HBM)] * hbm,
        scratch_shapes=scratch,
        compiler_params=pltpu.CompilerParams(vmem_limit_bytes=mib * 1024 * 1024),
    )


def shape(dims, dtype):
    return jax.ShapeDtypeStruct(dims, dtype)


def exchange(block, axis):
    return lax.all_to_all(block, axis, 0, 0, tiled=True)


def shards(entities, entity_state, relations, relation_state, heads, tails, rel_ids, negatives):
    bf, f32 = jnp.bfloat16, jnp.float32
    core = lax.axis_index("core").astype(jnp.int32).reshape(1)
    yl = lax.axis_index("yl").astype(jnp.int32).reshape(1)
    swap = [(0, 1), (1, 0)]
    before = [(i, (i - 1) % 64) for i in range(64)]
    after = [(i, (i + 1) % 64) for i in range(64)]
    edge = shape((D, EDGE), bf)

    own_b, code = call(start_kernel, (shape((D, COLS), bf), shape((CODES, EDGE), bf)), 0, 4, 60)(
        entities, tails, rel_ids, negatives
    )
    own = lax.all_gather(own_b, SRV, axis=1, tiled=True)
    two = lax.ppermute(call(heads_kernel, shape((D + CODES, EDGE), bf), 0, 3, 58)(own, heads, code), TRN, before)
    rel_b, h_one, gq_one, gown = call(first_kernel, (shape((RELS, D, D), bf), edge, edge, shape((D, PART), f32)), 0, 6, 24)(
        own, relations, heads, tails, rel_ids, negatives
    )
    rel_shape = (REL_ROWS, COLS)
    rel_mine, rel_send, q, gpos_q, weights, gq_two, tails_two = call(
        second_kernel,
        (shape(rel_shape, f32), shape(rel_shape, bf), edge, edge, shape((EDGE, PART), bf), edge, shape((1, EDGE), jnp.int32)),
        1,
        6,
        24,
    )(core, own, rel_b, rel_ids, h_one, gq_one, two)
    rel_got = lax.ppermute(rel_send, "core", swap)
    gq_two = lax.ppermute(gq_two, TRN, after)
    rel = call(relation_add_kernel, shape(rel_shape, bf), 0, 2)(rel_mine, rel_got)

    rel = exchange(rel.reshape(32, *PIECE), RING)
    ring_sum = call(ring_sum_kernel, shape((8, *PIECE), f32), 0, 1)(rel)

    rel = exchange(ring_sum, COLUMN)
    half = shape((4, D, COLS), bf)
    held = [pltpu.VMEM((D, EDGE), bf)] * 2 + [pltpu.VMEM((EDGE, PART), bf), pltpu.VMEM((D, PART), f32)]
    held = (*held, pltpu.SemaphoreType.DMA((4,)))
    mine, send = call(scatter_kernel, (half, half), 1, 5, 58, 5, held)(
        core, rel_b, heads, rel_ids, tails_two, gq_two, q, gpos_q, weights, gown, ring_sum
    )
    got = lax.all_gather(send, "core", axis=0, tiled=False)
    block, share = shape((D, COLS), f32), shape((D, COLS), bf)
    rel, keep, one, two, three = call(
        column_sum_kernel, (shape((32, *PIECE), bf), block, share, share, share), 2, 3
    )(yl, core, rel, mine, got)

    rel = exchange(rel, RING)
    one, two, three = [
        lax.ppermute(part, "yl", [(i, (i + k) % 4) for i in range(4)]) for k, part in ((1, one), (2, two), (3, three))
    ]
    new_entities, new_state = call(entity_kernel, (block, shape((1, COLS), f32)), 0, 6)(
        keep, one, two, three, entities, entity_state.reshape(1, COLS)
    )
    rel = lax.all_gather(rel.reshape(rel_shape), "core", axis=0, tiled=True)
    new_relations, new_rel_state = call(relation_kernel, (shape((RELS, D, D), f32), shape((RELS, D), f32)), 0, 3)(
        rel, relations, relation_state
    )
    return (new_entities, new_state.reshape(COLS), new_relations, new_rel_state)


def solution(mesh):
    fine = Mesh(mesh.devices.reshape(4, 2, 4, 8, 2), ("yl", "core", "x", "z", "yh"))
    every = TRN + SRV
    in_specs = (P(None, every), P(every), P(), P(), P(None, every), P(None, every), P(None, every), P(None, every, None))
    out_specs = (P(None, every), P(every), P(), P())
    return jax.shard_map(shards, mesh=fine, in_specs=in_specs, out_specs=out_specs, check_vma=False)
```

```python
import jax
import jax.numpy as jnp
from jax import lax
from jax.experimental import pallas as pl
from jax.experimental.pallas import tpu as pltpu
from jax.sharding import Mesh, PartitionSpec as P

learn_rate = 0.1

D = 400
RELS = 2
NEG = 1024
SPAN = 128
EDGE = 256
PART = 1024
COLS = 128
SRV = ("yl", "core")
TRN = ("x", "z", "yh")
STRIP = 56
CODES = 32
REL_ROWS = 1280
PIECE = (REL_ROWS // 32, COLS)
RING = ("x", "z")
COLUMN = ("yl", "yh")


def nn(a, b):
    return lax.dot_general(a, b, (((1,), (0,)), ((), ())), preferred_element_type=jnp.float32)


def nt(a, b):
    return lax.dot_general(a, b, (((1,), (1,)), ((), ())), preferred_element_type=jnp.float32)


def tn(a, b):
    return lax.dot_general(a, b, (((0,), (0,)), ((), ())), preferred_element_type=jnp.float32)


def one_hot(row, count):
    places = lax.broadcasted_iota(jnp.int32, (count, row.shape[1]), 0)
    return jnp.where(places == row, 1.0, 0.0).astype(jnp.bfloat16)


def neg_counts(row):
    high = one_hot(row // COLS, PART // COLS)
    low = one_hot(row % COLS, COLS)
    table = nt(high, low)
    return jnp.concatenate([table[i : i + 1, :] for i in range(PART // COLS)], axis=1)


def pack_relation(grad, out_ref):
    for group in range(3):
        out_ref[group * D : (group + 1) * D, :] = grad[:, group * COLS : (group + 1) * COLS].astype(out_ref.dtype)
    strip = grad[:, 3 * COLS :]
    packed = strip[:STRIP, :]
    for k in range(1, 8):
        piece = strip[k * STRIP : min((k + 1) * STRIP, D), :]
        if piece.shape[0] < STRIP:
            piece = jnp.concatenate([piece, jnp.zeros((STRIP - piece.shape[0], COLS), jnp.float32)], axis=0)
        packed = packed + pltpu.roll(piece, 16 * k, 1)
    packed = jnp.concatenate([packed, jnp.zeros((REL_ROWS - 3 * D - STRIP, COLS), jnp.float32)], axis=0)
    out_ref[3 * D : REL_ROWS, :] = packed.astype(out_ref.dtype)


def edge_grads(h, right, rel, rids, tails, negs):
    first = rids == 0
    t = nn(right, one_hot(tails, PART))
    q = jnp.where(first, tn(rel[0], h), tn(rel[1], h)).astype(jnp.bfloat16)
    qf = q.astype(jnp.float32)
    pos = jnp.sum(qf * t, axis=0, keepdims=True)
    gpos = -jax.nn.sigmoid(-pos)
    scores = tn(q, right)
    weights = []
    for c, row in enumerate(negs):
        counts = neg_counts(row) * (1.0 / NEG)
        weights.append((jax.nn.sigmoid(scores[c * SPAN : (c + 1) * SPAN, :]) * counts).astype(jnp.bfloat16))
    weights = jnp.concatenate(weights, axis=0)
    gq = (gpos * t + nt(right, weights)).astype(jnp.bfloat16)
    return q, (gpos * qf).astype(jnp.bfloat16), weights, gq


def gather_heads(own, heads):
    return nn(own, one_hot(heads, PART)).astype(jnp.bfloat16)


def right_grad(q, gpos_q, weights, tails):
    return nn(q, weights) + nt(gpos_q, one_hot(tails, PART))


def left_grad(gq, rel, rids, heads):
    gh = jnp.where(rids == 0, nn(rel[0], gq), nn(rel[1], gq)).astype(jnp.bfloat16)
    return nt(gh, one_hot(heads, PART))


def start_kernel(ent_ref, heads_ref, tails_ref, rids_ref, negs_ref, own_ref, code_ref):
    own_ref[...] = ent_ref[...].astype(jnp.bfloat16)
    rows = [tails_ref[1:2, :]]
    rows += [negs_ref[1, c : c + 1, k * EDGE : (k + 1) * EDGE] for c in range(2) for k in range(4)]
    rows.append(heads_ref[1:2, :])
    rows = [part for row in rows for part in (row // 32, row % 32)] + [rids_ref[1:2, :]]
    rows.append(jnp.zeros((CODES - len(rows), EDGE), jnp.int32))
    code_ref[...] = jnp.concatenate([row.astype(jnp.float32) for row in rows], axis=0).astype(jnp.bfloat16)


def decoded(code):
    code = code.astype(jnp.float32).astype(jnp.int32)
    return [code[2 * k : 2 * k + 1, :] * 32 + code[2 * k + 1 : 2 * k + 2, :] for k in range(10)], code[20:21, :]


def heads_kernel(own_ref, code_ref, out_ref):
    rows, _ = decoded(code_ref[...])
    out_ref[:D, :] = gather_heads(own_ref[...], rows[9])
    out_ref[D:, :] = code_ref[...]


def first_kernel(own_ref, rel_ref, heads_ref, tails_ref, rids_ref, negs_ref, rel_b_ref, h_ref, gq_ref, gown_ref):
    own = own_ref[...]
    rel = [rel_ref[r].astype(jnp.bfloat16) for r in range(RELS)]
    for r in range(RELS):
        rel_b_ref[r] = rel[r]
    heads, tails, rids = heads_ref[0:1, :], tails_ref[0:1, :], rids_ref[0:1, :]
    h = gather_heads(own, heads)
    q, gpos_q, weights, gq = edge_grads(h, own, rel, rids, tails, [negs_ref[0, c : c + 1, :] for c in range(2)])
    h_ref[...] = h
    gq_ref[...] = gq
    gown_ref[...] = right_grad(q, gpos_q, weights, tails) + left_grad(gq, rel, rids, heads)


def second_kernel(
    core_ref, own_ref, rel_ref, rids_ref, h_one_ref, gq_one_ref, two_ref,
    rel_mine_ref, rel_send_ref, q_ref, gpos_q_ref, weights_ref, gq_ref, tails_ref,
):
    h = two_ref[:D, :]
    rows, rids = decoded(two_ref[D:, :])
    tails = rows[0]
    negs = [jnp.concatenate(rows[1 + 4 * c : 5 + 4 * c], axis=1) for c in range(2)]
    tails_ref[...] = tails
    q, gpos_q, weights, gq = edge_grads(h, own_ref[...], rel_ref, rids, tails, negs)
    q_ref[...] = q
    gpos_q_ref[...] = gpos_q
    weights_ref[...] = weights
    gq_ref[...] = gq
    h = jnp.concatenate([h_one_ref[...], h], axis=1)
    gq = jnp.concatenate([gq_one_ref[...], gq], axis=1)
    gq = jnp.concatenate([gq, jnp.zeros((512 - D, 2 * EDGE), jnp.bfloat16)], axis=0)
    keep = jnp.concatenate([rids_ref[0:1, :], rids], axis=1) == core_ref[0]
    zero = jnp.zeros_like(h)
    pack_relation(nt(jnp.where(keep, h, zero), gq), rel_mine_ref)
    pack_relation(nt(jnp.where(keep, zero, h), gq), rel_send_ref)


def relation_add_kernel(core_ref, mine_ref, got_ref, out_ref):
    out_ref[...] = (mine_ref[...] + got_ref[1 - core_ref[0]].astype(jnp.float32)).astype(jnp.bfloat16)


def ring_sum_kernel(got_ref, _, out_ref):
    total = got_ref[0].astype(jnp.float32)
    for k in range(1, 32):
        total = total + got_ref[k].astype(jnp.float32)
    for k in range(8):
        out_ref[k] = total


def right_kernel(q_ref, gpos_q_ref, weights_ref, tails_ref, gown_ref, grad_ref):
    grad_ref[...] = gown_ref[...] + right_grad(q_ref[...], gpos_q_ref[...], weights_ref[...], tails_ref[...])


def left_kernel(core_ref, rel_ref, heads_ref, rids_ref, gq_ref, grad_hbm, _, mine_ref, send_ref, grad_ref, sem):
    even = core_ref[0] == 0
    copy = pltpu.make_async_copy(grad_hbm, grad_ref, sem)
    copy.start()
    grad = left_grad(gq_ref[...], rel_ref, rids_ref[1:2, :], heads_ref[1:2, :])
    copy.wait()
    grad = grad + grad_ref[...]
    for y in range(4):
        low = grad[:, 2 * y * COLS : (2 * y + 1) * COLS]
        high = grad[:, (2 * y + 1) * COLS : (2 * y + 2) * COLS]
        mine_ref[y] = jnp.where(even, low, high).astype(jnp.bfloat16)
        send_ref[y] = jnp.where(even, high, low).astype(jnp.bfloat16)


def column_sum_kernel(yl_ref, core_ref, rel_got_ref, mine_ref, got_ref, rel_ref, keep_ref, one_ref, two_ref, three_ref):
    total = rel_got_ref[0]
    for k in range(1, 8):
        total = total + rel_got_ref[k]
    total = total.astype(jnp.bfloat16)
    for k in range(32):
        rel_ref[k] = total
    for k, out_ref in enumerate((keep_ref, one_ref, two_ref, three_ref)):
        y = lax.rem(yl_ref[0] + k, 4)
        block = mine_ref[y].astype(jnp.float32) + got_ref[1 - core_ref[0], y].astype(jnp.float32)
        out_ref[...] = block.astype(out_ref.dtype)


def relation_kernel(grad_ref, rel_ref, state_ref, rel_out_ref, state_out_ref):
    for r in range(RELS):
        base = r * REL_ROWS
        groups = [grad_ref[base + g * D : base + (g + 1) * D, :].astype(jnp.float32) for g in range(3)]
        packed = grad_ref[base + 3 * D : base + REL_ROWS, :].astype(jnp.float32)[:STRIP, :]
        pieces = []
        for k in range(8):
            piece = packed if k == 0 else pltpu.roll(packed, COLS - 16 * k, 1)
            pieces.append(piece if (k + 1) * STRIP <= D else piece[: D - k * STRIP, :])
        strip = jnp.concatenate(pieces, axis=0)[:, :16]
        squares = groups[0] * groups[0] + groups[1] * groups[1] + groups[2] * groups[2]
        mean = (jnp.sum(squares, axis=1, keepdims=True) + jnp.sum(strip * strip, axis=1, keepdims=True)) * (1.0 / D)
        across = jnp.transpose(jnp.broadcast_to(mean, (D, COLS)))[0:1, :]
        state = state_ref[r : r + 1, :] + across
        state_out_ref[r : r + 1, :] = state
        scale = jnp.transpose(jnp.broadcast_to(learn_rate * lax.rsqrt(state), (8, D)))[:, 0:1]
        for g in range(3):
            cols = slice(g * COLS, (g + 1) * COLS)
            rel_out_ref[r, :, cols] = rel_ref[r, :, cols] - groups[g] * scale
        rel_out_ref[r, :, 3 * COLS :] = rel_ref[r, :, 3 * COLS :] - strip * scale


def entity_kernel(keep_ref, one_ref, two_ref, three_ref, ent_ref, state_ref, ent_out_ref, state_out_ref):
    total = keep_ref[...]
    for ref in (one_ref, two_ref, three_ref):
        total = total + ref[...].astype(jnp.float32)
    state = state_ref[...] + jnp.sum(total * total, axis=0, keepdims=True) * (1.0 / D)
    state_out_ref[...] = state
    ent_out_ref[...] = ent_ref[...] - total * (learn_rate * lax.rsqrt(state))


VMEM = pl.BlockSpec(memory_space=pltpu.VMEM)
SMEM = pl.BlockSpec(memory_space=pltpu.SMEM)


def call(kernel, outs, scalars, arrays, mib=8, hbm=0, scratch=()):
    return pl.pallas_call(
        kernel,
        out_shape=outs,
        in_specs=[SMEM] * scalars + [VMEM] * arrays + [pl.BlockSpec(memory_space=pltpu.HBM)] * hbm,
        scratch_shapes=scratch,
        compiler_params=pltpu.CompilerParams(vmem_limit_bytes=mib * 1024 * 1024),
    )


def shape(dims, dtype):
    return jax.ShapeDtypeStruct(dims, dtype)


def exchange(block, axis):
    return lax.all_to_all(block, axis, 0, 0, tiled=True)


def shards(entities, entity_state, relations, relation_state, heads, tails, rel_ids, negatives):
    bf, f32 = jnp.bfloat16, jnp.float32
    core = lax.axis_index("core").astype(jnp.int32).reshape(1)
    yl = lax.axis_index("yl").astype(jnp.int32).reshape(1)
    before = [(i, (i - 1) % 64) for i in range(64)]
    after = [(i, (i + 1) % 64) for i in range(64)]
    edge = shape((D, EDGE), bf)

    own_b, code = call(start_kernel, (shape((D, COLS), bf), shape((CODES, EDGE), bf)), 0, 5, 60)(
        entities, heads, tails, rel_ids, negatives
    )
    own = lax.all_gather(own_b, SRV, axis=1, tiled=True)
    two = lax.ppermute(call(heads_kernel, shape((D + CODES, EDGE), bf), 0, 2)(own, code), TRN, before)
    rel_b, h_one, gq_one, gown = call(first_kernel, (shape((RELS, D, D), bf), edge, edge, shape((D, PART), f32)), 0, 6, 24)(
        own, relations, heads, tails, rel_ids, negatives
    )
    rel_shape = (REL_ROWS, COLS)
    rel_mine, rel_send, q, gpos_q, weights, gq_two, tails_two = call(
        second_kernel,
        (shape(rel_shape, f32), shape(rel_shape, bf), edge, edge, shape((EDGE, PART), bf), edge, shape((1, EDGE), jnp.int32)),
        1,
        6,
        24,
    )(core, own, rel_b, rel_ids, h_one, gq_one, two)
    rel_got = lax.all_gather(rel_send, "core", axis=0, tiled=False)
    gq_two = lax.ppermute(gq_two, TRN, after)
    rel = call(relation_add_kernel, shape(rel_shape, bf), 1, 2)(core, rel_mine, rel_got)

    rel = exchange(rel.reshape(32, *PIECE), RING)
    grad = shape((D, PART), f32)
    grad = call(right_kernel, grad, 0, 5, 24)(q, gpos_q, weights, tails_two, gown)
    ring_sum = call(ring_sum_kernel, shape((8, *PIECE), f32), 0, 1, 8, 1)(rel, grad)

    rel = exchange(ring_sum, COLUMN)
    half = shape((4, D, COLS), bf)
    held = (pltpu.VMEM((D, PART), f32), pltpu.SemaphoreType.DMA)
    mine, send = call(left_kernel, (half, half), 1, 4, 58, 2, held)(core, rel_b, heads, rel_ids, gq_two, grad, ring_sum)
    got = lax.all_gather(send, "core", axis=0, tiled=False)
    block, share = shape((D, COLS), f32), shape((D, COLS), bf)
    rel, keep, one, two, three = call(
        column_sum_kernel, (shape((32, *PIECE), bf), block, share, share, share), 2, 3, 8
    )(yl, core, rel, mine, got)

    rel = exchange(rel, RING)
    one, two, three = [
        lax.ppermute(part, "yl", [(i, (i + k) % 4) for i in range(4)]) for k, part in ((1, one), (2, two), (3, three))
    ]
    new_entities, new_state = call(entity_kernel, (block, shape((1, COLS), f32)), 0, 6)(
        keep, one, two, three, entities, entity_state.reshape(1, COLS)
    )
    rel = lax.all_gather(rel.reshape(rel_shape), "core", axis=0, tiled=True)
    new_relations, new_rel_state = call(relation_kernel, (shape((RELS, D, D), f32), shape((RELS, D), f32)), 0, 3)(
        rel, relations, relation_state
    )
    return (new_entities, new_state.reshape(COLS), new_relations, new_rel_state)


def solution(mesh):
    fine = Mesh(mesh.devices.reshape(4, 2, 4, 8, 2), ("yl", "core", "x", "z", "yh"))
    every = TRN + SRV
    in_specs = (P(None, every), P(every), P(), P(), P(None, every), P(None, every), P(None, every), P(None, every, None))
    out_specs = (P(None, every), P(every), P(), P())
    return jax.shard_map(shards, mesh=fine, in_specs=in_specs, out_specs=out_specs, check_vma=False)
```

```python
import jax
import jax.numpy as jnp
from jax import lax
from jax.experimental import pallas as pl
from jax.experimental.pallas import tpu as pltpu
from jax.sharding import Mesh, PartitionSpec as P

learn_rate = 0.1

D = 400
RELS = 2
NEG = 1024
SPAN = 128
EDGE = 256
PART = 1024
COLS = 128
SRV = ("yl", "core")
TRN = ("x", "z", "yh")
STRIP = 56
CODES = 32
REL_ROWS = 1280
PIECE = (REL_ROWS // 32, COLS)
RING = ("x", "z")
COLUMN = ("yl", "yh")


def nn(a, b):
    return lax.dot_general(a, b, (((1,), (0,)), ((), ())), preferred_element_type=jnp.float32)


def nt(a, b):
    return lax.dot_general(a, b, (((1,), (1,)), ((), ())), preferred_element_type=jnp.float32)


def tn(a, b):
    return lax.dot_general(a, b, (((0,), (0,)), ((), ())), preferred_element_type=jnp.float32)


def one_hot(row, count):
    places = lax.broadcasted_iota(jnp.int32, (count, row.shape[1]), 0)
    return jnp.where(places == row, 1.0, 0.0).astype(jnp.bfloat16)


def neg_counts(row):
    high = one_hot(row // COLS, PART // COLS)
    low = one_hot(row % COLS, COLS)
    table = nt(high, low)
    return jnp.concatenate([table[i : i + 1, :] for i in range(PART // COLS)], axis=1)


def pack_relation(grad, out_ref):
    for group in range(3):
        out_ref[group * D : (group + 1) * D, :] = grad[:, group * COLS : (group + 1) * COLS].astype(out_ref.dtype)
    strip = grad[:, 3 * COLS :]
    packed = strip[:STRIP, :]
    for k in range(1, 8):
        piece = strip[k * STRIP : min((k + 1) * STRIP, D), :]
        if piece.shape[0] < STRIP:
            piece = jnp.concatenate([piece, jnp.zeros((STRIP - piece.shape[0], COLS), jnp.float32)], axis=0)
        packed = packed + pltpu.roll(piece, 16 * k, 1)
    packed = jnp.concatenate([packed, jnp.zeros((REL_ROWS - 3 * D - STRIP, COLS), jnp.float32)], axis=0)
    out_ref[3 * D : REL_ROWS, :] = packed.astype(out_ref.dtype)


def edge_grads(h, right, rel, rids, tails, negs):
    first = rids == 0
    t = nn(right, one_hot(tails, PART))
    q = jnp.where(first, tn(rel[0], h), tn(rel[1], h)).astype(jnp.bfloat16)
    qf = q.astype(jnp.float32)
    pos = jnp.sum(qf * t, axis=0, keepdims=True)
    gpos = -jax.nn.sigmoid(-pos)
    scores = tn(q, right)
    weights = []
    for c, row in enumerate(negs):
        counts = neg_counts(row) * (1.0 / NEG)
        weights.append((jax.nn.sigmoid(scores[c * SPAN : (c + 1) * SPAN, :]) * counts).astype(jnp.bfloat16))
    weights = jnp.concatenate(weights, axis=0)
    gq = (gpos * t + nt(right, weights)).astype(jnp.bfloat16)
    return q, (gpos * qf).astype(jnp.bfloat16), weights, gq


def gather_heads(own, heads):
    return nn(own, one_hot(heads, PART)).astype(jnp.bfloat16)


def right_grad(q, gpos_q, weights, tails):
    return nn(q, weights) + nt(gpos_q, one_hot(tails, PART))


def left_grad(gq, rel, rids, heads):
    gh = jnp.where(rids == 0, nn(rel[0], gq), nn(rel[1], gq)).astype(jnp.bfloat16)
    return nt(gh, one_hot(heads, PART))


def start_kernel(ent_ref, heads_ref, tails_ref, rids_ref, negs_ref, own_ref, code_ref):
    own_ref[...] = ent_ref[...].astype(jnp.bfloat16)
    rows = [tails_ref[1:2, :]]
    rows += [negs_ref[1, c : c + 1, k * EDGE : (k + 1) * EDGE] for c in range(2) for k in range(4)]
    rows.append(heads_ref[1:2, :])
    rows = [part for row in rows for part in (row // 32, row % 32)] + [rids_ref[1:2, :]]
    rows.append(jnp.zeros((CODES - len(rows), EDGE), jnp.int32))
    code_ref[...] = jnp.concatenate([row.astype(jnp.float32) for row in rows], axis=0).astype(jnp.bfloat16)


def decoded(code):
    code = code.astype(jnp.float32).astype(jnp.int32)
    return [code[2 * k : 2 * k + 1, :] * 32 + code[2 * k + 1 : 2 * k + 2, :] for k in range(10)], code[20:21, :]


def heads_kernel(own_ref, code_ref, out_ref):
    rows, _ = decoded(code_ref[...])
    out_ref[:D, :] = gather_heads(own_ref[...], rows[9])
    out_ref[D:, :] = code_ref[...]


def first_kernel(own_ref, rel_ref, heads_ref, tails_ref, rids_ref, negs_ref, rel_b_ref, h_ref, gq_ref, gown_ref):
    own = own_ref[...]
    rel = [rel_ref[r].astype(jnp.bfloat16) for r in range(RELS)]
    for r in range(RELS):
        rel_b_ref[r] = rel[r]
    heads, tails, rids = heads_ref[0:1, :], tails_ref[0:1, :], rids_ref[0:1, :]
    h = gather_heads(own, heads)
    q, gpos_q, weights, gq = edge_grads(h, own, rel, rids, tails, [negs_ref[0, c : c + 1, :] for c in range(2)])
    h_ref[...] = h
    gq_ref[...] = gq
    gown_ref[...] = right_grad(q, gpos_q, weights, tails) + left_grad(gq, rel, rids, heads)


def second_kernel(
    core_ref, own_ref, rel_ref, rids_ref, h_one_ref, gq_one_ref, two_ref,
    rel_mine_ref, rel_send_ref, q_ref, gpos_q_ref, weights_ref, gq_ref, tails_ref,
):
    h = two_ref[:D, :]
    rows, rids = decoded(two_ref[D:, :])
    tails = rows[0]
    negs = [jnp.concatenate(rows[1 + 4 * c : 5 + 4 * c], axis=1) for c in range(2)]
    tails_ref[...] = tails
    q, gpos_q, weights, gq = edge_grads(h, own_ref[...], rel_ref, rids, tails, negs)
    q_ref[...] = q
    gpos_q_ref[...] = gpos_q
    weights_ref[...] = weights
    gq_ref[...] = gq
    h = jnp.concatenate([h_one_ref[...], h], axis=1)
    gq = jnp.concatenate([gq_one_ref[...], gq], axis=1)
    gq = jnp.concatenate([gq, jnp.zeros((512 - D, 2 * EDGE), jnp.bfloat16)], axis=0)
    keep = jnp.concatenate([rids_ref[0:1, :], rids], axis=1) == core_ref[0]
    zero = jnp.zeros_like(h)
    pack_relation(nt(jnp.where(keep, h, zero), gq), rel_mine_ref)
    pack_relation(nt(jnp.where(keep, zero, h), gq), rel_send_ref)


def relation_add_kernel(core_ref, mine_ref, got_ref, out_ref):
    out_ref[...] = (mine_ref[...] + got_ref[1 - core_ref[0]].astype(jnp.float32)).astype(jnp.bfloat16)


def ring_sum_kernel(got_ref, out_ref):
    total = got_ref[0].astype(jnp.float32)
    for k in range(1, 32):
        total = total + got_ref[k].astype(jnp.float32)
    for k in range(8):
        out_ref[k] = total.astype(out_ref.dtype)


def right_kernel(
    tails_ref, q_hbm, gpos_q_hbm, weights_hbm, gown_hbm,
    grad_ref, q_ref, gpos_q_ref, weights_ref, gown_ref, sems,
):
    held = ((q_hbm, q_ref), (gpos_q_hbm, gpos_q_ref), (weights_hbm, weights_ref), (gown_hbm, gown_ref))
    copies = [pltpu.make_async_copy(src, dst, sems.at[k]) for k, (src, dst) in enumerate(held)]
    for copy in copies:
        copy.start()
    for copy in copies:
        copy.wait()
    grad_ref[...] = gown_ref[...] + right_grad(q_ref[...], gpos_q_ref[...], weights_ref[...], tails_ref[...])


def left_kernel(core_ref, rel_ref, heads_ref, rids_ref, gq_hbm, grad_hbm, _, mine_ref, send_ref, gq_ref, grad_ref, sems):
    even = core_ref[0] == 0
    copy_gq = pltpu.make_async_copy(gq_hbm, gq_ref, sems.at[0])
    copy = pltpu.make_async_copy(grad_hbm, grad_ref, sems.at[1])
    copy_gq.start()
    copy.start()
    copy_gq.wait()
    grad = left_grad(gq_ref[...], rel_ref, rids_ref[1:2, :], heads_ref[1:2, :])
    copy.wait()
    grad = grad + grad_ref[...]
    for y in range(4):
        low = grad[:, 2 * y * COLS : (2 * y + 1) * COLS]
        high = grad[:, (2 * y + 1) * COLS : (2 * y + 2) * COLS]
        mine_ref[y] = jnp.where(even, low, high).astype(jnp.bfloat16)
        send_ref[y] = jnp.where(even, high, low).astype(jnp.bfloat16)


def column_sum_kernel(yl_ref, core_ref, rel_got_ref, mine_ref, got_ref, rel_ref, keep_ref, one_ref, two_ref, three_ref):
    total = rel_got_ref[0].astype(jnp.float32)
    for k in range(1, 8):
        total = total + rel_got_ref[k].astype(jnp.float32)
    total = total.astype(jnp.bfloat16)
    for k in range(32):
        rel_ref[k] = total
    for k, out_ref in enumerate((keep_ref, one_ref, two_ref, three_ref)):
        y = lax.rem(yl_ref[0] + k, 4)
        block = mine_ref[y].astype(jnp.float32) + got_ref[1 - core_ref[0], y].astype(jnp.float32)
        out_ref[...] = block.astype(out_ref.dtype)


def relation_kernel(grad_ref, rel_ref, state_ref, rel_out_ref, state_out_ref):
    for r in range(RELS):
        base = r * REL_ROWS
        groups = [grad_ref[base + g * D : base + (g + 1) * D, :].astype(jnp.float32) for g in range(3)]
        packed = grad_ref[base + 3 * D : base + REL_ROWS, :].astype(jnp.float32)[:STRIP, :]
        pieces = []
        for k in range(8):
            piece = packed if k == 0 else pltpu.roll(packed, COLS - 16 * k, 1)
            pieces.append(piece if (k + 1) * STRIP <= D else piece[: D - k * STRIP, :])
        strip = jnp.concatenate(pieces, axis=0)[:, :16]
        squares = groups[0] * groups[0] + groups[1] * groups[1] + groups[2] * groups[2]
        mean = (jnp.sum(squares, axis=1, keepdims=True) + jnp.sum(strip * strip, axis=1, keepdims=True)) * (1.0 / D)
        across = jnp.transpose(jnp.broadcast_to(mean, (D, COLS)))[0:1, :]
        state = state_ref[r : r + 1, :] + across
        state_out_ref[r : r + 1, :] = state
        scale = jnp.transpose(jnp.broadcast_to(learn_rate * lax.rsqrt(state), (8, D)))[:, 0:1]
        for g in range(3):
            cols = slice(g * COLS, (g + 1) * COLS)
            rel_out_ref[r, :, cols] = rel_ref[r, :, cols] - groups[g] * scale
        rel_out_ref[r, :, 3 * COLS :] = rel_ref[r, :, 3 * COLS :] - strip * scale


def entity_kernel(keep_ref, one_ref, two_ref, three_ref, ent_ref, state_ref, ent_out_ref, state_out_ref):
    total = keep_ref[...]
    for ref in (one_ref, two_ref, three_ref):
        total = total + ref[...].astype(jnp.float32)
    state = state_ref[...] + jnp.sum(total * total, axis=0, keepdims=True) * (1.0 / D)
    state_out_ref[...] = state
    ent_out_ref[...] = ent_ref[...] - total * (learn_rate * lax.rsqrt(state))


VMEM = pl.BlockSpec(memory_space=pltpu.VMEM)
SMEM = pl.BlockSpec(memory_space=pltpu.SMEM)


def call(kernel, outs, scalars, arrays, mib=8, hbm=0, scratch=()):
    return pl.pallas_call(
        kernel,
        out_shape=outs,
        in_specs=[SMEM] * scalars + [VMEM] * arrays + [pl.BlockSpec(memory_space=pltpu.HBM)] * hbm,
        scratch_shapes=scratch,
        compiler_params=pltpu.CompilerParams(vmem_limit_bytes=mib * 1024 * 1024),
    )


def shape(dims, dtype):
    return jax.ShapeDtypeStruct(dims, dtype)


def exchange(block, axis):
    return lax.all_to_all(block, axis, 0, 0, tiled=True)


def shards(entities, entity_state, relations, relation_state, heads, tails, rel_ids, negatives):
    bf, f32 = jnp.bfloat16, jnp.float32
    core = lax.axis_index("core").astype(jnp.int32).reshape(1)
    yl = lax.axis_index("yl").astype(jnp.int32).reshape(1)
    before = [(i, (i - 1) % 64) for i in range(64)]
    after = [(i, (i + 1) % 64) for i in range(64)]
    edge = shape((D, EDGE), bf)

    own_b, code = call(start_kernel, (shape((D, COLS), bf), shape((CODES, EDGE), bf)), 0, 5, 60)(
        entities, heads, tails, rel_ids, negatives
    )
    own = lax.all_gather(own_b, SRV, axis=1, tiled=True)
    two = lax.ppermute(call(heads_kernel, shape((D + CODES, EDGE), bf), 0, 2)(own, code), TRN, before)
    rel_b, h_one, gq_one, gown = call(first_kernel, (shape((RELS, D, D), bf), edge, edge, shape((D, PART), f32)), 0, 6, 24)(
        own, relations, heads, tails, rel_ids, negatives
    )
    rel_shape = (REL_ROWS, COLS)
    rel_mine, rel_send, q, gpos_q, weights, gq_two, tails_two = call(
        second_kernel,
        (shape(rel_shape, f32), shape(rel_shape, bf), edge, edge, shape((EDGE, PART), bf), edge, shape((1, EDGE), jnp.int32)),
        1,
        6,
        24,
    )(core, own, rel_b, rel_ids, h_one, gq_one, two)
    rel_got = lax.all_gather(rel_send, "core", axis=0, tiled=False)
    gq_two = lax.ppermute(gq_two, TRN, after)
    rel = call(relation_add_kernel, shape(rel_shape, bf), 1, 2)(core, rel_mine, rel_got)

    rel = exchange(rel.reshape(32, *PIECE), RING)
    held = [pltpu.VMEM((D, EDGE), bf)] * 2 + [pltpu.VMEM((EDGE, PART), bf), pltpu.VMEM((D, PART), f32)]
    held = (*held, pltpu.SemaphoreType.DMA((4,)))
    grad = call(right_kernel, shape((D, PART), f32), 0, 1, 58, 4, held)(tails_two, q, gpos_q, weights, gown)
    ring_sum = call(ring_sum_kernel, shape((8, *PIECE), bf), 0, 1)(rel)

    rel = exchange(ring_sum, COLUMN)
    half = shape((4, D, COLS), bf)
    held = (pltpu.VMEM((D, EDGE), bf), pltpu.VMEM((D, PART), f32), pltpu.SemaphoreType.DMA((2,)))
    mine, send = call(left_kernel, (half, half), 1, 3, 58, 3, held)(core, rel_b, heads, rel_ids, gq_two, grad, ring_sum)
    got = lax.all_gather(send, "core", axis=0, tiled=False)
    block, share = shape((D, COLS), f32), shape((D, COLS), bf)
    rel, keep, one, two, three = call(
        column_sum_kernel, (shape((32, *PIECE), bf), block, share, share, share), 2, 3, 8
    )(yl, core, rel, mine, got)

    rel = exchange(rel, RING)
    one, two, three = [
        lax.ppermute(part, "yl", [(i, (i + k) % 4) for i in range(4)]) for k, part in ((1, one), (2, two), (3, three))
    ]
    new_entities, new_state = call(entity_kernel, (block, shape((1, COLS), f32)), 0, 6)(
        keep, one, two, three, entities, entity_state.reshape(1, COLS)
    )
    rel = lax.all_gather(rel.reshape(rel_shape), "core", axis=0, tiled=True)
    new_relations, new_rel_state = call(relation_kernel, (shape((RELS, D, D), f32), shape((RELS, D), f32)), 0, 3)(
        rel, relations, relation_state
    )
    return (new_entities, new_state.reshape(COLS), new_relations, new_rel_state)


def solution(mesh):
    fine = Mesh(mesh.devices.reshape(4, 2, 4, 8, 2), ("yl", "core", "x", "z", "yh"))
    every = TRN + SRV
    in_specs = (P(None, every), P(every), P(), P(), P(None, every), P(None, every), P(None, every), P(None, every, None))
    out_specs = (P(None, every), P(every), P(), P())
    return jax.shard_map(shards, mesh=fine, in_specs=in_specs, out_specs=out_specs, check_vma=False)
```

```python
import jax
import jax.numpy as jnp
from jax import lax
from jax.experimental import pallas as pl
from jax.experimental.pallas import tpu as pltpu
from jax.sharding import Mesh, PartitionSpec as P

learn_rate = 0.1

D = 400
RELS = 2
NEG = 1024
SPAN = 128
EDGE = 256
PART = 1024
COLS = 128
SRV = ("yl", "core")
TRN = ("x", "z", "yh")
STRIP = 56
CODES = 32
REL_ROWS = 1280
PIECE = (REL_ROWS // 32, COLS)
RING = ("x", "z")
COLUMN = ("yl", "yh")


def nn(a, b):
    return lax.dot_general(a, b, (((1,), (0,)), ((), ())), preferred_element_type=jnp.float32)


def nt(a, b):
    return lax.dot_general(a, b, (((1,), (1,)), ((), ())), preferred_element_type=jnp.float32)


def tn(a, b):
    return lax.dot_general(a, b, (((0,), (0,)), ((), ())), preferred_element_type=jnp.float32)


def one_hot(row, count):
    places = lax.broadcasted_iota(jnp.int32, (count, row.shape[1]), 0)
    return jnp.where(places == row, 1.0, 0.0).astype(jnp.bfloat16)


def neg_counts(row):
    high = one_hot(row // COLS, PART // COLS)
    low = one_hot(row % COLS, COLS)
    table = nt(high, low)
    return jnp.concatenate([table[i : i + 1, :] for i in range(PART // COLS)], axis=1)


def pack_relation(grad, out_ref):
    for group in range(3):
        out_ref[group * D : (group + 1) * D, :] = grad[:, group * COLS : (group + 1) * COLS].astype(out_ref.dtype)
    strip = grad[:, 3 * COLS :]
    packed = strip[:STRIP, :]
    for k in range(1, 8):
        piece = strip[k * STRIP : min((k + 1) * STRIP, D), :]
        if piece.shape[0] < STRIP:
            piece = jnp.concatenate([piece, jnp.zeros((STRIP - piece.shape[0], COLS), jnp.float32)], axis=0)
        packed = packed + pltpu.roll(piece, 16 * k, 1)
    packed = jnp.concatenate([packed, jnp.zeros((REL_ROWS - 3 * D - STRIP, COLS), jnp.float32)], axis=0)
    out_ref[3 * D : REL_ROWS, :] = packed.astype(out_ref.dtype)


def edge_grads(h, right, rel, rids, tails, negs):
    first = rids == 0
    t = nn(right, one_hot(tails, PART))
    q = jnp.where(first, tn(rel[0], h), tn(rel[1], h)).astype(jnp.bfloat16)
    qf = q.astype(jnp.float32)
    pos = jnp.sum(qf * t, axis=0, keepdims=True)
    gpos = -jax.nn.sigmoid(-pos)
    scores = tn(q, right)
    weights = []
    for c, row in enumerate(negs):
        counts = neg_counts(row) * (1.0 / NEG)
        weights.append((jax.nn.sigmoid(scores[c * SPAN : (c + 1) * SPAN, :]) * counts).astype(jnp.bfloat16))
    weights = jnp.concatenate(weights, axis=0)
    gq = (gpos * t + nt(right, weights)).astype(jnp.bfloat16)
    return q, (gpos * qf).astype(jnp.bfloat16), weights, gq


def gather_heads(own, heads):
    return nn(own, one_hot(heads, PART)).astype(jnp.bfloat16)


def right_grad(q, gpos_q, weights, tails):
    return nn(q, weights) + nt(gpos_q, one_hot(tails, PART))


def left_grad(gq, rel, rids, heads):
    gh = jnp.where(rids == 0, nn(rel[0], gq), nn(rel[1], gq)).astype(jnp.bfloat16)
    return nt(gh, one_hot(heads, PART))


def start_kernel(ent_ref, heads_ref, tails_ref, rids_ref, negs_ref, own_ref, code_ref):
    own_ref[...] = ent_ref[...].astype(jnp.bfloat16)
    rows = [tails_ref[1:2, :]]
    rows += [negs_ref[1, c : c + 1, k * EDGE : (k + 1) * EDGE] for c in range(2) for k in range(4)]
    rows.append(heads_ref[1:2, :])
    rows = [part for row in rows for part in (row // 32, row % 32)] + [rids_ref[1:2, :]]
    rows.append(jnp.zeros((CODES - len(rows), EDGE), jnp.int32))
    code_ref[...] = jnp.concatenate([row.astype(jnp.float32) for row in rows], axis=0).astype(jnp.bfloat16)


def decoded(code):
    code = code.astype(jnp.float32).astype(jnp.int32)
    return [code[2 * k : 2 * k + 1, :] * 32 + code[2 * k + 1 : 2 * k + 2, :] for k in range(10)], code[20:21, :]


def heads_kernel(own_ref, code_ref, out_ref):
    rows, _ = decoded(code_ref[...])
    out_ref[:D, :] = gather_heads(own_ref[...], rows[9])
    out_ref[D:, :] = code_ref[...]


def first_kernel(own_ref, rel_ref, heads_ref, tails_ref, rids_ref, negs_ref, rel_b_ref, h_ref, gq_ref, gown_ref):
    own = own_ref[...]
    rel = [rel_ref[r].astype(jnp.bfloat16) for r in range(RELS)]
    for r in range(RELS):
        rel_b_ref[r] = rel[r]
    heads, tails, rids = heads_ref[0:1, :], tails_ref[0:1, :], rids_ref[0:1, :]
    h = gather_heads(own, heads)
    q, gpos_q, weights, gq = edge_grads(h, own, rel, rids, tails, [negs_ref[0, c : c + 1, :] for c in range(2)])
    h_ref[...] = h
    gq_ref[...] = gq
    grad = right_grad(q, gpos_q, weights, tails) + left_grad(gq, rel, rids, heads)
    gown_ref[...] = grad.astype(jnp.bfloat16)


def second_kernel(
    core_ref, own_ref, rel_ref, rids_ref, h_one_ref, gq_one_ref, two_ref,
    rel_mine_ref, rel_send_ref, q_ref, gpos_q_ref, weights_ref, gq_ref, tails_ref,
):
    h = two_ref[:D, :]
    rows, rids = decoded(two_ref[D:, :])
    tails = rows[0]
    negs = [jnp.concatenate(rows[1 + 4 * c : 5 + 4 * c], axis=1) for c in range(2)]
    tails_ref[...] = tails
    q, gpos_q, weights, gq = edge_grads(h, own_ref[...], rel_ref, rids, tails, negs)
    q_ref[...] = q
    gpos_q_ref[...] = gpos_q
    weights_ref[...] = weights
    gq_ref[...] = gq
    h = jnp.concatenate([h_one_ref[...], h], axis=1)
    gq = jnp.concatenate([gq_one_ref[...], gq], axis=1)
    gq = jnp.concatenate([gq, jnp.zeros((512 - D, 2 * EDGE), jnp.bfloat16)], axis=0)
    keep = jnp.concatenate([rids_ref[0:1, :], rids], axis=1) == core_ref[0]
    zero = jnp.zeros_like(h)
    pack_relation(nt(jnp.where(keep, h, zero), gq), rel_mine_ref)
    pack_relation(nt(jnp.where(keep, zero, h), gq), rel_send_ref)


def relation_add_kernel(core_ref, mine_ref, got_ref, out_ref):
    out_ref[...] = (mine_ref[...] + got_ref[1 - core_ref[0]].astype(jnp.float32)).astype(jnp.bfloat16)


def ring_sum_kernel(_, got_ref, out_ref):
    total = got_ref[0].astype(jnp.float32)
    for k in range(1, 32):
        total = total + got_ref[k].astype(jnp.float32)
    for k in range(8):
        out_ref[k] = total.astype(out_ref.dtype)


def right_kernel(
    tails_ref, q_hbm, gpos_q_hbm, weights_hbm, gown_hbm,
    token_ref, grad_ref, q_ref, gpos_q_ref, weights_ref, gown_ref, sems,
):
    held = ((q_hbm, q_ref), (gpos_q_hbm, gpos_q_ref), (weights_hbm, weights_ref), (gown_hbm, gown_ref))
    copies = [pltpu.make_async_copy(src, dst, sems.at[k]) for k, (src, dst) in enumerate(held)]
    for copy in copies:
        copy.start()
    for copy in copies:
        copy.wait()
    token_ref[0] = 0
    grad = gown_ref[...].astype(jnp.float32) + right_grad(q_ref[...], gpos_q_ref[...], weights_ref[...], tails_ref[...])
    grad_ref[...] = grad.astype(jnp.bfloat16)


def left_kernel(core_ref, rel_ref, heads_ref, rids_ref, gq_hbm, grad_hbm, _, mine_ref, send_ref, gq_ref, grad_ref, sems):
    even = core_ref[0] == 0
    copy_gq = pltpu.make_async_copy(gq_hbm, gq_ref, sems.at[0])
    copy = pltpu.make_async_copy(grad_hbm, grad_ref, sems.at[1])
    copy_gq.start()
    copy.start()
    copy_gq.wait()
    grad = left_grad(gq_ref[...], rel_ref, rids_ref[1:2, :], heads_ref[1:2, :])
    copy.wait()
    grad = grad + grad_ref[...].astype(jnp.float32)
    for y in range(4):
        low = grad[:, 2 * y * COLS : (2 * y + 1) * COLS]
        high = grad[:, (2 * y + 1) * COLS : (2 * y + 2) * COLS]
        mine_ref[y] = jnp.where(even, low, high).astype(jnp.bfloat16)
        send_ref[y] = jnp.where(even, high, low).astype(jnp.bfloat16)


def column_sum_kernel(yl_ref, core_ref, rel_got_ref, mine_ref, got_ref, rel_ref, keep_ref, one_ref, two_ref, three_ref):
    total = rel_got_ref[0].astype(jnp.float32)
    for k in range(1, 8):
        total = total + rel_got_ref[k].astype(jnp.float32)
    total = total.astype(jnp.bfloat16)
    for k in range(32):
        rel_ref[k] = total
    for k, out_ref in enumerate((keep_ref, one_ref, two_ref, three_ref)):
        y = lax.rem(yl_ref[0] + k, 4)
        block = mine_ref[y].astype(jnp.float32) + got_ref[1 - core_ref[0], y].astype(jnp.float32)
        out_ref[...] = block.astype(out_ref.dtype)


def update_kernel(
    grad_ref, rel_ref, rel_state_ref, keep_ref, one_ref, two_ref, three_ref, ent_ref, state_ref,
    rel_out_ref, rel_state_out_ref, ent_out_ref, state_out_ref,
):
    for r in range(RELS):
        base = r * REL_ROWS
        groups = [grad_ref[base + g * D : base + (g + 1) * D, :].astype(jnp.float32) for g in range(3)]
        packed = grad_ref[base + 3 * D : base + REL_ROWS, :].astype(jnp.float32)[:STRIP, :]
        pieces = []
        for k in range(8):
            piece = packed if k == 0 else pltpu.roll(packed, COLS - 16 * k, 1)
            pieces.append(piece if (k + 1) * STRIP <= D else piece[: D - k * STRIP, :])
        strip = jnp.concatenate(pieces, axis=0)[:, :16]
        squares = groups[0] * groups[0] + groups[1] * groups[1] + groups[2] * groups[2]
        mean = (jnp.sum(squares, axis=1, keepdims=True) + jnp.sum(strip * strip, axis=1, keepdims=True)) * (1.0 / D)
        across = jnp.transpose(jnp.broadcast_to(mean, (D, COLS)))[0:1, :]
        state = rel_state_ref[r : r + 1, :] + across
        rel_state_out_ref[r : r + 1, :] = state
        scale = jnp.transpose(jnp.broadcast_to(learn_rate * lax.rsqrt(state), (8, D)))[:, 0:1]
        for g in range(3):
            cols = slice(g * COLS, (g + 1) * COLS)
            rel_out_ref[r, :, cols] = rel_ref[r, :, cols] - groups[g] * scale
        rel_out_ref[r, :, 3 * COLS :] = rel_ref[r, :, 3 * COLS :] - strip * scale
    total = keep_ref[...]
    for ref in (one_ref, two_ref, three_ref):
        total = total + ref[...].astype(jnp.float32)
    state = state_ref[...] + jnp.sum(total * total, axis=0, keepdims=True) * (1.0 / D)
    state_out_ref[...] = state
    ent_out_ref[...] = ent_ref[...] - total * (learn_rate * lax.rsqrt(state))


VMEM = pl.BlockSpec(memory_space=pltpu.VMEM)
SMEM = pl.BlockSpec(memory_space=pltpu.SMEM)


def call(kernel, outs, scalars, arrays, mib=8, hbm=0, scratch=(), out_specs=None):
    return pl.pallas_call(
        kernel,
        out_shape=outs,
        in_specs=[SMEM] * scalars + [VMEM] * arrays + [pl.BlockSpec(memory_space=pltpu.HBM)] * hbm,
        scratch_shapes=scratch,
        **({} if out_specs is None else {"out_specs": out_specs}),
        compiler_params=pltpu.CompilerParams(vmem_limit_bytes=mib * 1024 * 1024),
    )


def shape(dims, dtype):
    return jax.ShapeDtypeStruct(dims, dtype)


def exchange(block, axis):
    return lax.all_to_all(block, axis, 0, 0, tiled=True)


def shards(entities, entity_state, relations, relation_state, heads, tails, rel_ids, negatives):
    bf, f32 = jnp.bfloat16, jnp.float32
    core = lax.axis_index("core").astype(jnp.int32).reshape(1)
    yl = lax.axis_index("yl").astype(jnp.int32).reshape(1)
    before = [(i, (i - 1) % 64) for i in range(64)]
    after = [(i, (i + 1) % 64) for i in range(64)]
    edge = shape((D, EDGE), bf)

    own_b, code = call(start_kernel, (shape((D, COLS), bf), shape((CODES, EDGE), bf)), 0, 5, 60)(
        entities, heads, tails, rel_ids, negatives
    )
    own = lax.all_gather(own_b, SRV, axis=1, tiled=True)
    two = lax.ppermute(call(heads_kernel, shape((D + CODES, EDGE), bf), 0, 2)(own, code), TRN, before)
    rel_b, h_one, gq_one, gown = call(first_kernel, (shape((RELS, D, D), bf), edge, edge, shape((D, PART), bf)), 0, 6, 24)(
        own, relations, heads, tails, rel_ids, negatives
    )
    rel_shape = (REL_ROWS, COLS)
    rel_mine, rel_send, q, gpos_q, weights, gq_two, tails_two = call(
        second_kernel,
        (shape(rel_shape, f32), shape(rel_shape, bf), edge, edge, shape((EDGE, PART), bf), edge, shape((1, EDGE), jnp.int32)),
        1,
        6,
        24,
    )(core, own, rel_b, rel_ids, h_one, gq_one, two)
    rel_got = lax.all_gather(rel_send, "core", axis=0, tiled=False)
    gq_two = lax.ppermute(gq_two, TRN, after)
    rel = call(relation_add_kernel, shape(rel_shape, bf), 1, 2)(core, rel_mine, rel_got)

    rel = exchange(rel.reshape(32, *PIECE), RING)
    held = [pltpu.VMEM((D, EDGE), bf)] * 2 + [pltpu.VMEM((EDGE, PART), bf), pltpu.VMEM((D, PART), bf)]
    held = (*held, pltpu.SemaphoreType.DMA((4,)))
    token, grad = call(
        right_kernel, (shape((1,), jnp.int32), shape((D, PART), bf)), 0, 1, 58, 4, held, [SMEM, VMEM]
    )(tails_two, q, gpos_q, weights, gown)
    ring_sum = call(ring_sum_kernel, shape((8, *PIECE), f32), 1, 1)(token, rel)

    rel = exchange(ring_sum, COLUMN)
    half = shape((4, D, COLS), bf)
    held = (pltpu.VMEM((D, EDGE), bf), pltpu.VMEM((D, PART), bf), pltpu.SemaphoreType.DMA((2,)))
    mine, send = call(left_kernel, (half, half), 1, 3, 58, 3, held)(core, rel_b, heads, rel_ids, gq_two, grad, ring_sum)
    got = lax.all_gather(send, "core", axis=0, tiled=False)
    block, share = shape((D, COLS), f32), shape((D, COLS), bf)
    rel, keep, one, two, three = call(
        column_sum_kernel, (shape((32, *PIECE), bf), block, share, share, share), 2, 3, 8
    )(yl, core, rel, mine, got)

    rel = exchange(rel, RING)
    one, two, three = [
        lax.ppermute(part, "yl", [(i, (i + k) % 4) for i in range(4)]) for k, part in ((1, one), (2, two), (3, three))
    ]
    rel = lax.all_gather(rel.reshape(rel_shape), "core", axis=0, tiled=True)
    new_relations, new_rel_state, new_entities, new_state = call(
        update_kernel, (shape((RELS, D, D), f32), shape((RELS, D), f32), block, shape((1, COLS), f32)), 0, 9
    )(rel, relations, relation_state, keep, one, two, three, entities, entity_state.reshape(1, COLS))
    return (new_entities, new_state.reshape(COLS), new_relations, new_rel_state)


def solution(mesh):
    fine = Mesh(mesh.devices.reshape(4, 2, 4, 8, 2), ("yl", "core", "x", "z", "yh"))
    every = TRN + SRV
    in_specs = (P(None, every), P(every), P(), P(), P(None, every), P(None, every), P(None, every), P(None, every, None))
    out_specs = (P(None, every), P(every), P(), P())
    return jax.shard_map(shards, mesh=fine, in_specs=in_specs, out_specs=out_specs, check_vma=False)
```

```python
import jax
import jax.numpy as jnp
from jax import lax
from jax.experimental import pallas as pl
from jax.experimental.pallas import tpu as pltpu
from jax.sharding import Mesh, PartitionSpec as P

learn_rate = 0.1

D = 400
RELS = 2
NEG = 1024
SPAN = 128
EDGE = 256
PART = 1024
COLS = 128
SRV = ("yl", "core")
TRN = ("x", "z", "yh")
STRIP = 56
CODES = 32
REL_ROWS = 1280
PIECE = (REL_ROWS // 32, COLS)
RING = ("x", "z")
COLUMN = ("yl", "yh")


def nn(a, b):
    return lax.dot_general(a, b, (((1,), (0,)), ((), ())), preferred_element_type=jnp.float32)


def nt(a, b):
    return lax.dot_general(a, b, (((1,), (1,)), ((), ())), preferred_element_type=jnp.float32)


def tn(a, b):
    return lax.dot_general(a, b, (((0,), (0,)), ((), ())), preferred_element_type=jnp.float32)


def one_hot(row, count):
    places = lax.broadcasted_iota(jnp.int32, (count, row.shape[1]), 0)
    return jnp.where(places == row, 1.0, 0.0).astype(jnp.bfloat16)


def neg_counts(row):
    high = one_hot(row // COLS, PART // COLS)
    low = one_hot(row % COLS, COLS)
    table = nt(high, low)
    return jnp.concatenate([table[i : i + 1, :] for i in range(PART // COLS)], axis=1)


def pack_relation(grad, out_ref):
    for group in range(3):
        out_ref[group * D : (group + 1) * D, :] = grad[:, group * COLS : (group + 1) * COLS].astype(out_ref.dtype)
    strip = grad[:, 3 * COLS :]
    packed = strip[:STRIP, :]
    for k in range(1, 8):
        piece = strip[k * STRIP : min((k + 1) * STRIP, D), :]
        if piece.shape[0] < STRIP:
            piece = jnp.concatenate([piece, jnp.zeros((STRIP - piece.shape[0], COLS), jnp.float32)], axis=0)
        packed = packed + pltpu.roll(piece, 16 * k, 1)
    packed = jnp.concatenate([packed, jnp.zeros((REL_ROWS - 3 * D - STRIP, COLS), jnp.float32)], axis=0)
    out_ref[3 * D : REL_ROWS, :] = packed.astype(out_ref.dtype)


def edge_grads(h, right, rel, rids, tails, negs):
    first = rids == 0
    t = nn(right, one_hot(tails, PART))
    q = jnp.where(first, tn(rel[0], h), tn(rel[1], h)).astype(jnp.bfloat16)
    qf = q.astype(jnp.float32)
    pos = jnp.sum(qf * t, axis=0, keepdims=True)
    gpos = -jax.nn.sigmoid(-pos)
    scores = tn(q, right)
    weights = []
    for c, row in enumerate(negs):
        counts = neg_counts(row) * (1.0 / NEG)
        weights.append((jax.nn.sigmoid(scores[c * SPAN : (c + 1) * SPAN, :]) * counts).astype(jnp.bfloat16))
    weights = jnp.concatenate(weights, axis=0)
    gq = (gpos * t + nt(right, weights)).astype(jnp.bfloat16)
    return q, (gpos * qf).astype(jnp.bfloat16), weights, gq


def gather_heads(own, heads):
    return nn(own, one_hot(heads, PART)).astype(jnp.bfloat16)


def right_grad(q, gpos_q, weights, tails):
    return nn(q, weights) + nt(gpos_q, one_hot(tails, PART))


def head_grads(gq, rel, rids):
    return jnp.where(rids == 0, nn(rel[0], gq), nn(rel[1], gq)).astype(jnp.bfloat16)


def left_grad(gh, heads):
    return nt(gh, one_hot(heads, PART))


def start_kernel(ent_ref, heads_ref, tails_ref, rids_ref, negs_ref, own_ref, code_ref):
    own_ref[...] = ent_ref[...].astype(jnp.bfloat16)
    rows = [tails_ref[1:2, :]]
    rows += [negs_ref[1, c : c + 1, k * EDGE : (k + 1) * EDGE] for c in range(2) for k in range(4)]
    rows.append(heads_ref[1:2, :])
    rows = [part for row in rows for part in (row // 32, row % 32)] + [rids_ref[1:2, :]]
    rows.append(jnp.zeros((CODES - len(rows), EDGE), jnp.int32))
    code_ref[...] = jnp.concatenate([row.astype(jnp.float32) for row in rows], axis=0).astype(jnp.bfloat16)


def decoded(code):
    code = code.astype(jnp.float32).astype(jnp.int32)
    return [code[2 * k : 2 * k + 1, :] * 32 + code[2 * k + 1 : 2 * k + 2, :] for k in range(10)], code[20:21, :]


def heads_kernel(own_ref, code_ref, out_ref):
    rows, _ = decoded(code_ref[...])
    out_ref[:D, :] = gather_heads(own_ref[...], rows[9])
    out_ref[D:, :] = code_ref[...]


def first_kernel(own_ref, rel_ref, heads_ref, tails_ref, rids_ref, negs_ref, rel_b_ref, h_ref, gq_ref, gown_ref):
    own = own_ref[...]
    rel = [rel_ref[r].astype(jnp.bfloat16) for r in range(RELS)]
    for r in range(RELS):
        rel_b_ref[r] = rel[r]
    heads, tails, rids = heads_ref[0:1, :], tails_ref[0:1, :], rids_ref[0:1, :]
    h = gather_heads(own, heads)
    q, gpos_q, weights, gq = edge_grads(h, own, rel, rids, tails, [negs_ref[0, c : c + 1, :] for c in range(2)])
    h_ref[...] = h
    gq_ref[...] = gq
    grad = right_grad(q, gpos_q, weights, tails) + left_grad(head_grads(gq, rel, rids), heads)
    gown_ref[...] = grad.astype(jnp.bfloat16)


def second_kernel(
    core_ref, own_ref, rel_ref, rids_ref, h_one_ref, gq_one_ref, two_ref,
    rel_mine_ref, rel_send_ref, q_ref, gpos_q_ref, weights_ref, gh_ref, tails_ref,
):
    h = two_ref[:D, :]
    rows, rids = decoded(two_ref[D:, :])
    tails = rows[0]
    negs = [jnp.concatenate(rows[1 + 4 * c : 5 + 4 * c], axis=1) for c in range(2)]
    tails_ref[...] = tails
    q, gpos_q, weights, gq = edge_grads(h, own_ref[...], rel_ref, rids, tails, negs)
    q_ref[...] = q
    gpos_q_ref[...] = gpos_q
    weights_ref[...] = weights
    gh_ref[...] = head_grads(gq, rel_ref, rids)
    h = jnp.concatenate([h_one_ref[...], h], axis=1)
    gq = jnp.concatenate([gq_one_ref[...], gq], axis=1)
    gq = jnp.concatenate([gq, jnp.zeros((512 - D, 2 * EDGE), jnp.bfloat16)], axis=0)
    keep = jnp.concatenate([rids_ref[0:1, :], rids], axis=1) == core_ref[0]
    zero = jnp.zeros_like(h)
    pack_relation(nt(jnp.where(keep, h, zero), gq), rel_mine_ref)
    pack_relation(nt(jnp.where(keep, zero, h), gq), rel_send_ref)


def relation_add_kernel(core_ref, mine_ref, got_ref, out_ref):
    out_ref[...] = (mine_ref[...] + got_ref[1 - core_ref[0]].astype(jnp.float32)).astype(jnp.bfloat16)


def ring_sum_kernel(got_ref, out_ref):
    total = got_ref[0].astype(jnp.float32)
    for k in range(1, 32):
        total = total + got_ref[k].astype(jnp.float32)
    for k in range(8):
        out_ref[k] = total.astype(out_ref.dtype)


def right_kernel(
    tails_ref, q_hbm, gpos_q_hbm, weights_hbm, gown_hbm,
    grad_ref, q_ref, gpos_q_ref, weights_ref, gown_ref, sems,
):
    held = ((q_hbm, q_ref), (gpos_q_hbm, gpos_q_ref), (weights_hbm, weights_ref), (gown_hbm, gown_ref))
    copies = [pltpu.make_async_copy(src, dst, sems.at[k]) for k, (src, dst) in enumerate(held)]
    for copy in copies:
        copy.start()
    for copy in copies:
        copy.wait()
    grad = gown_ref[...].astype(jnp.float32) + right_grad(q_ref[...], gpos_q_ref[...], weights_ref[...], tails_ref[...])
    grad_ref[...] = grad.astype(jnp.bfloat16)


def left_kernel(core_ref, heads_ref, gh_hbm, grad_hbm, _, mine_ref, send_ref, gh_ref, grad_ref, sems):
    even = core_ref[0] == 0
    copy_gh = pltpu.make_async_copy(gh_hbm, gh_ref, sems.at[0])
    copy = pltpu.make_async_copy(grad_hbm, grad_ref, sems.at[1])
    copy_gh.start()
    copy.start()
    copy_gh.wait()
    grad = left_grad(gh_ref[...], heads_ref[1:2, :])
    copy.wait()
    grad = grad + grad_ref[...].astype(jnp.float32)
    for y in range(4):
        low = grad[:, 2 * y * COLS : (2 * y + 1) * COLS]
        high = grad[:, (2 * y + 1) * COLS : (2 * y + 2) * COLS]
        mine_ref[y] = jnp.where(even, low, high).astype(jnp.bfloat16)
        send_ref[y] = jnp.where(even, high, low).astype(jnp.bfloat16)


def column_sum_kernel(yl_ref, core_ref, rel_got_ref, mine_ref, got_ref, rel_ref, keep_ref, one_ref, two_ref, three_ref):
    total = rel_got_ref[0].astype(jnp.float32)
    for k in range(1, 8):
        total = total + rel_got_ref[k].astype(jnp.float32)
    total = total.astype(jnp.bfloat16)
    for k in range(32):
        rel_ref[k] = total
    for k, out_ref in enumerate((keep_ref, one_ref, two_ref, three_ref)):
        y = lax.rem(yl_ref[0] + k, 4)
        block = mine_ref[y].astype(jnp.float32) + got_ref[1 - core_ref[0], y].astype(jnp.float32)
        out_ref[...] = block.astype(out_ref.dtype)


def update_kernel(
    grad_ref, rel_ref, rel_state_ref, keep_ref, one_ref, two_ref, three_ref, ent_ref, state_ref,
    rel_out_ref, rel_state_out_ref, ent_out_ref, state_out_ref,
):
    for r in range(RELS):
        base = r * REL_ROWS
        groups = [grad_ref[base + g * D : base + (g + 1) * D, :].astype(jnp.float32) for g in range(3)]
        packed = grad_ref[base + 3 * D : base + REL_ROWS, :].astype(jnp.float32)[:STRIP, :]
        pieces = []
        for k in range(8):
            piece = packed if k == 0 else pltpu.roll(packed, COLS - 16 * k, 1)
            pieces.append(piece if (k + 1) * STRIP <= D else piece[: D - k * STRIP, :])
        strip = jnp.concatenate(pieces, axis=0)[:, :16]
        squares = groups[0] * groups[0] + groups[1] * groups[1] + groups[2] * groups[2]
        mean = (jnp.sum(squares, axis=1, keepdims=True) + jnp.sum(strip * strip, axis=1, keepdims=True)) * (1.0 / D)
        across = jnp.transpose(jnp.broadcast_to(mean, (D, COLS)))[0:1, :]
        state = rel_state_ref[r : r + 1, :] + across
        rel_state_out_ref[r : r + 1, :] = state
        scale = jnp.transpose(jnp.broadcast_to(learn_rate * lax.rsqrt(state), (8, D)))[:, 0:1]
        for g in range(3):
            cols = slice(g * COLS, (g + 1) * COLS)
            rel_out_ref[r, :, cols] = rel_ref[r, :, cols] - groups[g] * scale
        rel_out_ref[r, :, 3 * COLS :] = rel_ref[r, :, 3 * COLS :] - strip * scale
    total = keep_ref[...]
    for ref in (one_ref, two_ref, three_ref):
        total = total + ref[...].astype(jnp.float32)
    state = state_ref[...] + jnp.sum(total * total, axis=0, keepdims=True) * (1.0 / D)
    state_out_ref[...] = state
    ent_out_ref[...] = ent_ref[...] - total * (learn_rate * lax.rsqrt(state))


VMEM = pl.BlockSpec(memory_space=pltpu.VMEM)
SMEM = pl.BlockSpec(memory_space=pltpu.SMEM)


def call(kernel, outs, scalars, arrays, mib=8, hbm=0, scratch=()):
    return pl.pallas_call(
        kernel,
        out_shape=outs,
        in_specs=[SMEM] * scalars + [VMEM] * arrays + [pl.BlockSpec(memory_space=pltpu.HBM)] * hbm,
        scratch_shapes=scratch,
        compiler_params=pltpu.CompilerParams(vmem_limit_bytes=mib * 1024 * 1024),
    )


def shape(dims, dtype):
    return jax.ShapeDtypeStruct(dims, dtype)


def exchange(block, axis):
    return lax.all_to_all(block, axis, 0, 0, tiled=True)


def shards(entities, entity_state, relations, relation_state, heads, tails, rel_ids, negatives):
    bf, f32 = jnp.bfloat16, jnp.float32
    core = lax.axis_index("core").astype(jnp.int32).reshape(1)
    yl = lax.axis_index("yl").astype(jnp.int32).reshape(1)
    before = [(i, (i - 1) % 64) for i in range(64)]
    after = [(i, (i + 1) % 64) for i in range(64)]
    edge = shape((D, EDGE), bf)

    own_b, code = call(start_kernel, (shape((D, COLS), bf), shape((CODES, EDGE), bf)), 0, 5, 60)(
        entities, heads, tails, rel_ids, negatives
    )
    own = lax.all_gather(own_b, SRV, axis=1, tiled=True)
    two = lax.ppermute(call(heads_kernel, shape((D + CODES, EDGE), bf), 0, 2)(own, code), TRN, before)
    rel_b, h_one, gq_one, gown = call(first_kernel, (shape((RELS, D, D), bf), edge, edge, shape((D, PART), bf)), 0, 6, 24)(
        own, relations, heads, tails, rel_ids, negatives
    )
    rel_shape = (REL_ROWS, COLS)
    rel_mine, rel_send, q, gpos_q, weights, gh, tails_two = call(
        second_kernel,
        (shape(rel_shape, f32), shape(rel_shape, bf), edge, edge, shape((EDGE, PART), bf), edge, shape((1, EDGE), jnp.int32)),
        1,
        6,
        24,
    )(core, own, rel_b, rel_ids, h_one, gq_one, two)
    rel_got = lax.all_gather(rel_send, "core", axis=0, tiled=False)
    gh = lax.ppermute(gh, TRN, after)
    rel = call(relation_add_kernel, shape(rel_shape, bf), 1, 2)(core, rel_mine, rel_got)

    rel = exchange(rel.reshape(32, *PIECE), RING)
    held = [pltpu.VMEM((D, EDGE), bf)] * 2 + [pltpu.VMEM((EDGE, PART), bf), pltpu.VMEM((D, PART), bf)]
    held = (*held, pltpu.SemaphoreType.DMA((4,)))
    grad = call(right_kernel, shape((D, PART), bf), 0, 1, 58, 4, held)(tails_two, q, gpos_q, weights, gown)
    ring_sum = call(ring_sum_kernel, shape((8, *PIECE), bf), 0, 1)(rel)

    rel = exchange(ring_sum, COLUMN)
    half = shape((4, D, COLS), bf)
    held = (pltpu.VMEM((D, EDGE), bf), pltpu.VMEM((D, PART), bf), pltpu.SemaphoreType.DMA((2,)))
    mine, send = call(left_kernel, (half, half), 1, 1, 58, 3, held)(core, heads, gh, grad, ring_sum)
    got = lax.all_gather(send, "core", axis=0, tiled=False)
    block, share = shape((D, COLS), f32), shape((D, COLS), bf)
    rel, keep, one, two, three = call(
        column_sum_kernel, (shape((32, *PIECE), bf), block, share, share, share), 2, 3, 8
    )(yl, core, rel, mine, got)

    rel = exchange(rel, RING)
    one, two, three = [
        lax.ppermute(part, "yl", [(i, (i + k) % 4) for i in range(4)]) for k, part in ((1, one), (2, two), (3, three))
    ]
    rel = lax.all_gather(rel.reshape(rel_shape), "core", axis=0, tiled=True)
    new_relations, new_rel_state, new_entities, new_state = call(
        update_kernel, (shape((RELS, D, D), f32), shape((RELS, D), f32), block, shape((1, COLS), f32)), 0, 9
    )(rel, relations, relation_state, keep, one, two, three, entities, entity_state.reshape(1, COLS))
    return (new_entities, new_state.reshape(COLS), new_relations, new_rel_state)


def solution(mesh):
    fine = Mesh(mesh.devices.reshape(4, 2, 4, 8, 2), ("yl", "core", "x", "z", "yh"))
    every = TRN + SRV
    in_specs = (P(None, every), P(every), P(), P(), P(None, every), P(None, every), P(None, every), P(None, every, None))
    out_specs = (P(None, every), P(every), P(), P())
    return jax.shard_map(shards, mesh=fine, in_specs=in_specs, out_specs=out_specs, check_vma=False)
```

```python
import jax
import jax.numpy as jnp
from jax import lax
from jax.experimental import pallas as pl
from jax.experimental.pallas import tpu as pltpu
from jax.sharding import Mesh, PartitionSpec as P

learn_rate = 0.1

D = 400
RELS = 2
NEG = 1024
SPAN = 128
EDGE = 256
PART = 1024
COLS = 128
SRV = ("yl", "core")
TRN = ("x", "z", "yh")
STRIP = 56
CODES = 32
REL_ROWS = 1280
PIECE = (REL_ROWS // 32, COLS)
RING = ("x", "z")
COLUMN = ("yl", "yh")


def nn(a, b):
    return lax.dot_general(a, b, (((1,), (0,)), ((), ())), preferred_element_type=jnp.float32)


def nt(a, b):
    return lax.dot_general(a, b, (((1,), (1,)), ((), ())), preferred_element_type=jnp.float32)


def tn(a, b):
    return lax.dot_general(a, b, (((0,), (0,)), ((), ())), preferred_element_type=jnp.float32)


def one_hot(row, count):
    places = lax.broadcasted_iota(jnp.int32, (count, row.shape[1]), 0)
    return jnp.where(places == row, 1.0, 0.0).astype(jnp.bfloat16)


def neg_counts(row):
    high = one_hot(row // COLS, PART // COLS)
    low = one_hot(row % COLS, COLS)
    table = nt(high, low)
    return jnp.concatenate([table[i : i + 1, :] for i in range(PART // COLS)], axis=1)


def pack_relation(grad, out_ref):
    for group in range(3):
        out_ref[group * D : (group + 1) * D, :] = grad[:, group * COLS : (group + 1) * COLS].astype(out_ref.dtype)
    strip = grad[:, 3 * COLS :]
    packed = strip[:STRIP, :]
    for k in range(1, 8):
        piece = strip[k * STRIP : min((k + 1) * STRIP, D), :]
        if piece.shape[0] < STRIP:
            piece = jnp.concatenate([piece, jnp.zeros((STRIP - piece.shape[0], COLS), jnp.float32)], axis=0)
        packed = packed + pltpu.roll(piece, 16 * k, 1)
    packed = jnp.concatenate([packed, jnp.zeros((REL_ROWS - 3 * D - STRIP, COLS), jnp.float32)], axis=0)
    out_ref[3 * D : REL_ROWS, :] = packed.astype(out_ref.dtype)


def edge_grads(h, right, rel, rids, tails, negs):
    first = rids == 0
    t = nn(right, one_hot(tails, PART))
    q = jnp.where(first, tn(rel[0], h), tn(rel[1], h)).astype(jnp.bfloat16)
    qf = q.astype(jnp.float32)
    pos = jnp.sum(qf * t, axis=0, keepdims=True)
    gpos = -jax.nn.sigmoid(-pos)
    scores = tn(q, right)
    weights = []
    for c, row in enumerate(negs):
        counts = neg_counts(row) * (1.0 / NEG)
        weights.append((jax.nn.sigmoid(scores[c * SPAN : (c + 1) * SPAN, :]) * counts).astype(jnp.bfloat16))
    weights = jnp.concatenate(weights, axis=0)
    gq = (gpos * t + nt(right, weights)).astype(jnp.bfloat16)
    return q, (gpos * qf).astype(jnp.bfloat16), weights, gq


def gather_heads(own, heads):
    return nn(own, one_hot(heads, PART)).astype(jnp.bfloat16)


def right_grad(q, gpos_q, weights, tails):
    return nn(q, weights) + nt(gpos_q, one_hot(tails, PART))


def head_grads(gq, rel, rids):
    return jnp.where(rids == 0, nn(rel[0], gq), nn(rel[1], gq)).astype(jnp.bfloat16)


def left_grad(gh, heads):
    return nt(gh, one_hot(heads, PART))


def start_kernel(ent_ref, heads_ref, tails_ref, rids_ref, negs_ref, own_ref, code_ref):
    own_ref[...] = ent_ref[...].astype(jnp.bfloat16)
    rows = [tails_ref[1:2, :]]
    rows += [negs_ref[1, c : c + 1, k * EDGE : (k + 1) * EDGE] for c in range(2) for k in range(4)]
    rows.append(heads_ref[1:2, :])
    rows = [part for row in rows for part in (row // 32, row % 32)] + [rids_ref[1:2, :]]
    rows.append(jnp.zeros((CODES - len(rows), EDGE), jnp.int32))
    code_ref[...] = jnp.concatenate([row.astype(jnp.float32) for row in rows], axis=0).astype(jnp.bfloat16)


def decoded(code):
    code = code.astype(jnp.float32).astype(jnp.int32)
    return [code[2 * k : 2 * k + 1, :] * 32 + code[2 * k + 1 : 2 * k + 2, :] for k in range(10)], code[20:21, :]


def heads_kernel(own_ref, code_ref, out_ref):
    rows, _ = decoded(code_ref[...])
    out_ref[:D, :] = gather_heads(own_ref[...], rows[9])
    out_ref[D:, :] = code_ref[...]


def first_kernel(own_ref, rel_ref, heads_ref, tails_ref, rids_ref, negs_ref, rel_b_ref, h_ref, gq_ref, gown_ref):
    own = own_ref[...]
    rel = [rel_ref[r].astype(jnp.bfloat16) for r in range(RELS)]
    for r in range(RELS):
        rel_b_ref[r] = rel[r]
    heads, tails, rids = heads_ref[0:1, :], tails_ref[0:1, :], rids_ref[0:1, :]
    h = gather_heads(own, heads)
    q, gpos_q, weights, gq = edge_grads(h, own, rel, rids, tails, [negs_ref[0, c : c + 1, :] for c in range(2)])
    h_ref[...] = h
    gq_ref[...] = gq
    grad = right_grad(q, gpos_q, weights, tails) + left_grad(head_grads(gq, rel, rids), heads)
    gown_ref[...] = grad.astype(jnp.bfloat16)


def second_kernel(
    core_ref, own_ref, rel_ref, rids_ref, h_one_ref, gq_one_ref, two_ref,
    rel_mine_ref, rel_send_ref, q_ref, gpos_q_ref, weights_ref, gh_ref, tails_ref,
):
    h = two_ref[:D, :]
    rows, rids = decoded(two_ref[D:, :])
    tails = rows[0]
    negs = [jnp.concatenate(rows[1 + 4 * c : 5 + 4 * c], axis=1) for c in range(2)]
    tails_ref[...] = tails
    q, gpos_q, weights, gq = edge_grads(h, own_ref[...], rel_ref, rids, tails, negs)
    q_ref[...] = q
    gpos_q_ref[...] = gpos_q
    weights_ref[...] = weights
    gh_ref[...] = head_grads(gq, rel_ref, rids)
    h = jnp.concatenate([h_one_ref[...], h], axis=1)
    gq = jnp.concatenate([gq_one_ref[...], gq], axis=1)
    gq = jnp.concatenate([gq, jnp.zeros((512 - D, 2 * EDGE), jnp.bfloat16)], axis=0)
    keep = jnp.concatenate([rids_ref[0:1, :], rids], axis=1) == core_ref[0]
    zero = jnp.zeros_like(h)
    pack_relation(nt(jnp.where(keep, h, zero), gq), rel_mine_ref)
    pack_relation(nt(jnp.where(keep, zero, h), gq), rel_send_ref)


def relation_add_kernel(core_ref, mine_ref, got_ref, out_ref):
    out_ref[...] = (mine_ref[...] + got_ref[1 - core_ref[0]].astype(jnp.float32)).astype(jnp.bfloat16)


def ring_sum_kernel(got_ref, out_ref):
    total = got_ref[0].astype(jnp.float32)
    for k in range(1, 32):
        total = total + got_ref[k].astype(jnp.float32)
    for k in range(8):
        out_ref[k] = total.astype(out_ref.dtype)


def right_kernel(
    tails_ref, q_hbm, gpos_q_hbm, weights_hbm, gown_hbm,
    grad_ref, q_ref, gpos_q_ref, weights_ref, gown_ref, sems,
):
    held = ((q_hbm, q_ref), (gpos_q_hbm, gpos_q_ref), (weights_hbm, weights_ref), (gown_hbm, gown_ref))
    copies = [pltpu.make_async_copy(src, dst, sems.at[k]) for k, (src, dst) in enumerate(held)]
    for copy in copies:
        copy.start()
    for copy in copies:
        copy.wait()
    grad = gown_ref[...].astype(jnp.float32) + right_grad(q_ref[...], gpos_q_ref[...], weights_ref[...], tails_ref[...])
    grad_ref[...] = grad.astype(jnp.bfloat16)


def left_kernel(core_ref, heads_ref, gh_hbm, grad_hbm, _, mine_ref, send_ref, gh_ref, grad_ref, sems):
    even = core_ref[0] == 0
    copy_gh = pltpu.make_async_copy(gh_hbm, gh_ref, sems.at[0])
    copy = pltpu.make_async_copy(grad_hbm, grad_ref, sems.at[1])
    copy_gh.start()
    copy.start()
    copy_gh.wait()
    grad = left_grad(gh_ref[...], heads_ref[1:2, :])
    copy.wait()
    grad = grad + grad_ref[...].astype(jnp.float32)
    for y in range(4):
        low = grad[:, 2 * y * COLS : (2 * y + 1) * COLS]
        high = grad[:, (2 * y + 1) * COLS : (2 * y + 2) * COLS]
        mine_ref[y] = jnp.where(even, low, high).astype(jnp.bfloat16)
        send_ref[y] = jnp.where(even, high, low).astype(jnp.bfloat16)


def column_sum_kernel(yl_ref, core_ref, rel_got_ref, mine_ref, got_ref, rel_ref, keep_ref, one_ref, two_ref, three_ref):
    total = rel_got_ref[0].astype(jnp.float32)
    for k in range(1, 8):
        total = total + rel_got_ref[k].astype(jnp.float32)
    total = total.astype(jnp.bfloat16)
    for k in range(32):
        rel_ref[k] = total
    for k, out_ref in enumerate((keep_ref, one_ref, two_ref, three_ref)):
        y = lax.rem(yl_ref[0] + k, 4)
        block = mine_ref[y].astype(jnp.float32) + got_ref[1 - core_ref[0], y].astype(jnp.float32)
        out_ref[...] = block.astype(out_ref.dtype)


def update_kernel(
    grad_ref, rel_ref, rel_state_ref, keep_ref, one_ref, two_ref, three_ref, ent_ref, state_ref,
    rel_out_hbm, rel_state_out_ref, ent_out_ref, state_out_ref, rel_out_ref, sems,
):
    copies = [pltpu.make_async_copy(rel_out_ref.at[r], rel_out_hbm.at[r], sems.at[r]) for r in range(RELS)]
    for r in range(RELS):
        base = r * REL_ROWS
        groups = [grad_ref[base + g * D : base + (g + 1) * D, :].astype(jnp.float32) for g in range(3)]
        packed = grad_ref[base + 3 * D : base + REL_ROWS, :].astype(jnp.float32)[:STRIP, :]
        pieces = []
        for k in range(8):
            piece = packed if k == 0 else pltpu.roll(packed, COLS - 16 * k, 1)
            pieces.append(piece if (k + 1) * STRIP <= D else piece[: D - k * STRIP, :])
        strip = jnp.concatenate(pieces, axis=0)[:, :16]
        squares = groups[0] * groups[0] + groups[1] * groups[1] + groups[2] * groups[2]
        mean = (jnp.sum(squares, axis=1, keepdims=True) + jnp.sum(strip * strip, axis=1, keepdims=True)) * (1.0 / D)
        across = jnp.transpose(jnp.broadcast_to(mean, (D, COLS)))[0:1, :]
        state = rel_state_ref[r : r + 1, :] + across
        rel_state_out_ref[r : r + 1, :] = state
        scale = jnp.transpose(jnp.broadcast_to(learn_rate * lax.rsqrt(state), (8, D)))[:, 0:1]
        for g in range(3):
            cols = slice(g * COLS, (g + 1) * COLS)
            rel_out_ref[r, :, cols] = rel_ref[r, :, cols] - groups[g] * scale
        rel_out_ref[r, :, 3 * COLS :] = rel_ref[r, :, 3 * COLS :] - strip * scale
        copies[r].start()
    total = keep_ref[...]
    for ref in (one_ref, two_ref, three_ref):
        total = total + ref[...].astype(jnp.float32)
    state = state_ref[...] + jnp.sum(total * total, axis=0, keepdims=True) * (1.0 / D)
    state_out_ref[...] = state
    ent_out_ref[...] = ent_ref[...] - total * (learn_rate * lax.rsqrt(state))
    for copy in copies:
        copy.wait()


VMEM = pl.BlockSpec(memory_space=pltpu.VMEM)
SMEM = pl.BlockSpec(memory_space=pltpu.SMEM)


def call(kernel, outs, scalars, arrays, mib=8, hbm=0, scratch=(), out_specs=None):
    return pl.pallas_call(
        kernel,
        out_shape=outs,
        in_specs=[SMEM] * scalars + [VMEM] * arrays + [pl.BlockSpec(memory_space=pltpu.HBM)] * hbm,
        scratch_shapes=scratch,
        **({} if out_specs is None else {"out_specs": out_specs}),
        compiler_params=pltpu.CompilerParams(vmem_limit_bytes=mib * 1024 * 1024),
    )


def shape(dims, dtype):
    return jax.ShapeDtypeStruct(dims, dtype)


def exchange(block, axis):
    return lax.all_to_all(block, axis, 0, 0, tiled=True)


def shards(entities, entity_state, relations, relation_state, heads, tails, rel_ids, negatives):
    bf, f32 = jnp.bfloat16, jnp.float32
    core = lax.axis_index("core").astype(jnp.int32).reshape(1)
    yl = lax.axis_index("yl").astype(jnp.int32).reshape(1)
    before = [(i, (i - 1) % 64) for i in range(64)]
    after = [(i, (i + 1) % 64) for i in range(64)]
    edge = shape((D, EDGE), bf)

    own_b, code = call(start_kernel, (shape((D, COLS), bf), shape((CODES, EDGE), bf)), 0, 5, 60)(
        entities, heads, tails, rel_ids, negatives
    )
    own = lax.all_gather(own_b, SRV, axis=1, tiled=True)
    two = lax.ppermute(call(heads_kernel, shape((D + CODES, EDGE), bf), 0, 2)(own, code), TRN, before)
    rel_b, h_one, gq_one, gown = call(first_kernel, (shape((RELS, D, D), bf), edge, edge, shape((D, PART), bf)), 0, 6, 24)(
        own, relations, heads, tails, rel_ids, negatives
    )
    rel_shape = (REL_ROWS, COLS)
    rel_mine, rel_send, q, gpos_q, weights, gh, tails_two = call(
        second_kernel,
        (shape(rel_shape, f32), shape(rel_shape, bf), edge, edge, shape((EDGE, PART), bf), edge, shape((1, EDGE), jnp.int32)),
        1,
        6,
        24,
    )(core, own, rel_b, rel_ids, h_one, gq_one, two)
    rel_got = lax.all_gather(rel_send, "core", axis=0, tiled=False)
    gh = lax.ppermute(gh, TRN, after)
    rel = call(relation_add_kernel, shape(rel_shape, bf), 1, 2)(core, rel_mine, rel_got)

    rel = exchange(rel.reshape(32, *PIECE), RING)
    held = [pltpu.VMEM((D, EDGE), bf)] * 2 + [pltpu.VMEM((EDGE, PART), bf), pltpu.VMEM((D, PART), bf)]
    held = (*held, pltpu.SemaphoreType.DMA((4,)))
    grad = call(right_kernel, shape((D, PART), bf), 0, 1, 58, 4, held)(tails_two, q, gpos_q, weights, gown)
    ring_sum = call(ring_sum_kernel, shape((8, *PIECE), bf), 0, 1)(rel)

    rel = exchange(ring_sum, COLUMN)
    half = shape((4, D, COLS), bf)
    held = (pltpu.VMEM((D, EDGE), bf), pltpu.VMEM((D, PART), bf), pltpu.SemaphoreType.DMA((2,)))
    mine, send = call(left_kernel, (half, half), 1, 1, 58, 3, held)(core, heads, gh, grad, ring_sum)
    got = lax.all_gather(send, "core", axis=0, tiled=False)
    block, share = shape((D, COLS), f32), shape((D, COLS), bf)
    rel, keep, one, two, three = call(
        column_sum_kernel, (shape((32, *PIECE), bf), block, share, share, share), 2, 3, 8
    )(yl, core, rel, mine, got)

    rel = exchange(rel, RING)
    one, two, three = [
        lax.ppermute(part, "yl", [(i, (i + k) % 4) for i in range(4)]) for k, part in ((1, one), (2, two), (3, three))
    ]
    rel = lax.all_gather(rel.reshape(rel_shape), "core", axis=0, tiled=True)
    new_relations, new_rel_state, new_entities, new_state = call(
        update_kernel,
        (shape((RELS, D, D), f32), shape((RELS, D), f32), block, shape((1, COLS), f32)),
        0,
        9,
        8,
        0,
        (pltpu.VMEM((RELS, D, D), f32), pltpu.SemaphoreType.DMA((RELS,))),
        [pl.BlockSpec(memory_space=pltpu.HBM), VMEM, VMEM, VMEM],
    )(rel, relations, relation_state, keep, one, two, three, entities, entity_state.reshape(1, COLS))
    return (new_entities, new_state.reshape(COLS), new_relations, new_rel_state)


def solution(mesh):
    fine = Mesh(mesh.devices.reshape(4, 2, 4, 8, 2), ("yl", "core", "x", "z", "yh"))
    every = TRN + SRV
    in_specs = (P(None, every), P(every), P(), P(), P(None, every), P(None, every), P(None, every), P(None, every, None))
    out_specs = (P(None, every), P(every), P(), P())
    return jax.shard_map(shards, mesh=fine, in_specs=in_specs, out_specs=out_specs, check_vma=False)
```
